128 devices in a mesh: dp: 8 (over y, x_lo), seq: 16 (over z, x_hi, core).
Axes of the slice: x: 4 (x_hi: 2, x_lo: 2; x = x_hi * 2 + x_lo), y: 4, z: 4, core: 2. Of those that a mesh axis runs over, the one named last changes fastest.
Arguments:
- slides: float32 [8, 2, 2048, 768], P('dp', None, 'seq'), may hold values from -6 to 6
- counts: int32 [8], P('dp'), may hold values from 1 to 2, as said below
- levels: int32 [16], replicated, may hold values from 0 to 4, as said below
- norm_gain: float32 [768], replicated, may hold values from 0.1 to 1.9
- w_qkv: float32 [768, 2304], replicated
- w_out: float32 [768, 768], replicated, may hold values from -0.875 to 0.875
- cotangent: float32 [8, 2, 2048, 768], P('dp', None, 'seq'), may hold values from -6 to 6
Outputs:
- branch: float32 [8, 2, 2048, 768], P('dp', None, 'seq')
- input_grad: float32 [8, 2, 2048, 768], P('dp', None, 'seq')
- grad_gain: float32 [768], P('seq')
- grad_qkv: float32 [768, 2304], P(None, 'seq')
- grad_out: float32 [768, 768], P(None, 'seq')
The draws below stay inside these ranges and needn't reach their ends.
Inputs may be any that keep to these rules, and one draw needn't show every extreme that they name: `counts`: number of live slots of each group; slots from it on are padding; some group has 2 and some has 1. `levels`: every level from 0 to 4 is used by some head.
All inputs are finite; a program needn't handle non-finite values.
Results may differ from the reference program's by a relative error of at most 0.0003.
Values sent between devices are 32-bit elements; how exact they have to be, the bound alone decides.
No kernel may reach another device: no remote copies, remote signals or barrier semaphores. Data moves between devices by JAX's collectives and lax.ppermute only.
A program may use at most 320 MiB of HBM per device.

```python
import math
from functools import partial
import jax
import jax.numpy as jnp
from jax import lax

D = 768
HEADS = 16
HDIM = 48
SLIDES = 2
LEVELS = 5
SEG0 = 512
GROUPS = 8
LENGTH = 2048


def draw_counts(key, part):
    key = jax.random.fold_in(key, 11)
    key_a, key_b = jax.random.split(key)
    numbers = jax.random.randint(key_a, (GROUPS,), 1, SLIDES + 1)
    reorder_heads = jax.random.permutation(key_b, GROUPS)
    numbers = numbers.at[reorder_heads[0]].set(SLIDES).at[reorder_heads[1]].set(1)
    return numbers.astype(jnp.int32)


def draw_levels(key, part):
    key = jax.random.fold_in(key, 23)
    reorder_heads = jax.random.permutation(key, HEADS)
    return (reorder_heads % LEVELS).astype(jnp.int32)


def draw_w_qkv(key, part):
    key = jax.random.fold_in(key, 37)
    keys_all = jax.random.split(key, 1)
    base_w = jax.random.normal(keys_all[0], (D, 3 * D), jnp.float32) / math.sqrt(D)
    return base_w


def level_of(stream_key, dims, cuts, low, top_value):
    def one(axis_at, parts):
        draws = jax.random.uniform(jax.random.fold_in(jax.random.fold_in(stream_key, 6), axis_at), (parts,), jnp.float32, low / len(cuts), top_value / len(cuts))
        return jnp.repeat(jnp.exp(draws), dims[axis_at] // parts).reshape((-1,) + (1,) * (len(dims) - axis_at - 1))

    level = one(*cuts[0])
    for cut in cuts[1:]:
        level = level * one(*cut)
    return level


def scatter_about(rng, shape, deviation, limit, pieces=(), held_as=jnp.bfloat16):
    loudness = level_of(rng, shape, pieces, -0.22, 0.18) if pieces else 1.0
    array = jax.random.normal(rng, shape, jnp.float32) * deviation * loudness
    return jnp.minimum(jnp.maximum(array, -limit), limit).astype(held_as)


def setup_inputs(seed: int = 0) -> dict:
    streams_of = jax.random.split(jax.random.key(seed), 8)
    slides = scatter_about(streams_of[0], (GROUPS, SLIDES, LENGTH, D), 1.0, 6.0, ((0, 8), (2, 16)), jnp.float32)
    counts = draw_counts(jax.random.fold_in(streams_of[7], 71), 0)
    levels = draw_levels(jax.random.fold_in(streams_of[7], 71), 0)
    norm_gain = jnp.clip(1.0 + 0.18 * jax.random.normal(streams_of[3], (D,), jnp.float32), 0.1, 1.9)
    w_qkv = draw_w_qkv(jax.random.fold_in(streams_of[7], 71), 0)
    w_out = scatter_about(streams_of[5], (D, D), (D // 16) ** -0.5, 0.875, (), jnp.float32)
    cotangent = scatter_about(streams_of[6], (GROUPS, SLIDES, LENGTH, D), 1.0, 6.0, ((0, 8), (2, 16)), jnp.float32)
    return {"slides": slides, "counts": counts, "levels": levels, "norm_gain": norm_gain, "w_qkv": w_qkv, "w_out": w_out, "cotangent": cotangent}


HIGH = lax.Precision.HIGHEST
EPS = 1e-05

def attend_rate(q, k, v, start_shift, rate, seg_first):
    length, width = q.shape
    picked = length // rate
    span = min(seg_first, picked)

    def select(x):
        rows = lax.dynamic_index_in_dim(x.reshape(picked, rate, width), start_shift, axis=1, keepdims=False)
        return rows.reshape(picked // span, span, width)
    query_g = select(q)
    key_g = select(k)
    value_g = select(v)
    scores = jnp.einsum('gid,gjd->gij', query_g, key_g, precision=HIGH) * width ** (-0.5)
    row_max = lax.optimization_barrier(jnp.max(scores, axis=-1, keepdims=True))
    expo = jnp.exp(scores - row_max)
    softmax_w = expo / lax.optimization_barrier(jnp.sum(expo, axis=-1, keepdims=True))
    group_out = jnp.einsum('gij,gjd->gid', softmax_w, value_g, precision=HIGH).reshape(picked, 1, width)
    frame = jnp.zeros((picked, rate, width), q.dtype)
    return lax.dynamic_update_slice_in_dim(frame, group_out, start_shift, axis=1).reshape(length, width)

def attend_head(q, k, v, dilation_level, head_number, seg_first):
    dilation_level = dilation_level.astype(jnp.int32)
    dilation_factor = jnp.left_shift(jnp.int32(1), dilation_level)
    start_shift = (head_number.astype(jnp.int32) % dilation_factor).astype(jnp.int32)
    options = [partial(attend_rate, rate=2 ** lev, seg_first=seg_first) for lev in range(LEVELS)]
    return lax.switch(dilation_level, options, q, k, v, start_shift)

def attend_all(q, k, v, head_levels, head_ids):

    def per_head(items):
        return attend_head(items[0], items[1], items[2], items[3], items[4], SEG0)
    result = lax.map(per_head, (jnp.swapaxes(q, 0, 1), jnp.swapaxes(k, 0, 1), jnp.swapaxes(v, 0, 1), head_levels, head_ids))
    return jnp.swapaxes(result, 0, 1)

def attn_layer(values, norm_gain, w_qkv, w_out, levels):
    mean_val = lax.optimization_barrier(jnp.mean(values, axis=-1, keepdims=True))
    centred = values - mean_val
    spread_sq = lax.optimization_barrier(jnp.mean(centred * centred, axis=-1, keepdims=True))
    normed = centred * lax.rsqrt(spread_sq + EPS) * norm_gain
    qkv_rows = jnp.dot(normed, w_qkv, precision=HIGH)
    length = values.shape[0]
    split = qkv_rows.reshape(length, 3, HEADS, HDIM)
    head_ids = jnp.arange(HEADS, dtype=jnp.int32)
    attended = attend_all(split[:, 0], split[:, 1], split[:, 2], levels, head_ids)
    return jnp.dot(attended.reshape(length, D), w_out, precision=HIGH)

def reference(slides, counts, levels, norm_gain, w_qkv, w_out, cotangent):
    active_flag = (jnp.arange(SLIDES, dtype=jnp.int32)[None, :] < counts[:, None]).astype(jnp.float32).reshape(-1)
    inputs = slides.reshape(GROUPS * SLIDES, LENGTH, D)
    cot_rows = cotangent.reshape(GROUPS * SLIDES, LENGTH, D)

    def one(running, sample):
        values, cot_one, use_one = sample

        def forward(a, b, c, e):
            return attn_layer(a, b, c, e, levels)
        branch, back_fn = jax.vjp(forward, values, norm_gain, w_qkv, w_out)
        input_gradient, grad_g, grad_q, grad_o = back_fn(cot_one * use_one)
        running = (running[0] + grad_g, running[1] + grad_q, running[2] + grad_o)
        return (running, (branch * use_one, input_gradient))
    zero_grads = (jnp.zeros((D,), jnp.float32), jnp.zeros((D, 3 * D), jnp.float32), jnp.zeros((D, D), jnp.float32))
    totals, (branch, input_grad) = lax.scan(one, zero_grads, (inputs, cot_rows, active_flag))
    return (branch.reshape(GROUPS, SLIDES, LENGTH, D), input_grad.reshape(GROUPS, SLIDES, LENGTH, D), totals[0], totals[1], totals[2])
```

```python
from functools import partial

import jax
import jax.numpy as jnp
from jax import lax
from jax.experimental import pallas as pl
from jax.experimental.pallas import tpu as pltpu
from jax.sharding import PartitionSpec as P

HEADS = 16
HDIM = 48
LEVELS = 5
EPS = 1e-05
ROWS = 128
WIDTH = 768
HALF = 384
SCALE = HDIM**-0.5
F32 = jnp.float32
BF16 = jnp.bfloat16
VMEM_LIMIT = 60 * 1024 * 1024


def split(x):
    hi = x.astype(BF16)
    return hi, (x - hi.astype(F32)).astype(BF16)


def dot(a, b, dims=((1,), (0,))):
    return lax.dot_general(a, b, (dims, ((), ())), preferred_element_type=F32)


def dot_stack(a2, w, dims=((1,), (0,))):
    m = a2.shape[0] // 2
    wh, wl = split(w)
    both = dot(a2, wh, dims)
    return both[:m] + both[m:] + dot(a2[:m], wl, dims)


def stack(x):
    return jnp.concatenate(split(x), axis=0)


def normalise(x):
    mean = jnp.mean(x, axis=-1, keepdims=True)
    centred = x - mean
    rstd = lax.rsqrt(jnp.mean(centred * centred, axis=-1, keepdims=True) + EPS)
    return centred * rstd, rstd


def live_rows(counts):
    rows = lax.broadcasted_iota(jnp.int32, (2 * ROWS, 1), 0)
    return (rows < counts[0] * ROWS).astype(F32)


def roll_half(x):
    return pltpu.roll(x, 64, 1)


def left_lanes(shape):
    return lax.broadcasted_iota(jnp.int32, shape, 1) < 64


def pack_kernel(cap, levels, offs, counts, x, cot, gain, wq, wk, wv, wo, out, tiles, n2, c2):
    g = pl.program_id(0)

    @pl.when(g == 0)
    def _():
        xhat, _ = normalise(x[...].reshape(2 * ROWS, WIDTH))
        n2[...] = stack(xhat * gain[...])
        c2[...] = stack(cot[...].reshape(2 * ROWS, WIDTH) * live_rows(counts))

    q = dot_stack(n2[...], wq[...])
    k = dot_stack(n2[...], wk[...])
    v = dot_stack(n2[...], wv[...])
    do = dot_stack(c2[...], wo[...], ((1,), (1,)))
    for i in range(8):
        lanes = slice(HDIM * i, HDIM * (i + 1))
        at = (g * 8 + i) * 3
        tails = []
        for s in range(2):
            rows = slice(ROWS * s, ROWS * (s + 1))
            vs = v[rows, lanes]
            tiles[at + 2 * s] = jnp.concatenate([q[rows, lanes], k[rows, lanes], vs[:, :32]], axis=1)
            tails += [vs[:, 32:], do[rows, lanes]]
        tiles[at + 1] = jnp.concatenate(tails, axis=1)

    @pl.when(g == 1)
    def _():
        def one(h, carry):
            level, off = levels[h], offs[h]
            for lev in range(LEVELS):
                n, rate = ROWS >> lev, 1 << lev

                @pl.when(level == lev)
                def _():
                    dst = off // cap
                    if n > cap:
                        for s in range(2):
                            a = tiles[h * 3 + 2 * s]
                            b = tiles[h * 3 + 1]
                            out[dst + s, 0] = a[:cap]
                            out[dst + s, 2] = a[cap:]
                            top, low = b[:cap], b[cap:]
                            pick = left_lanes(top.shape)
                            if s == 0:
                                out[dst + s, 1] = jnp.where(pick, top, roll_half(low))
                            else:
                                out[dst + s, 1] = jnp.where(pick, roll_half(top), low)
                    else:
                        row = pl.multiple_of(off % cap, 8)
                        first = h % rate
                        for j in range(3):
                            src = pl.ds(first, n, stride=rate) if rate > 1 else pl.ds(0, n)
                            out[dst, j, pl.ds(row, n), :] = tiles[h * 3 + j, src, :]

            return carry

        lax.fori_loop(0, HEADS, one, 0)


def pack(cap, levels, offs, counts, x, cot, gain, w_qkv, w_out):
    smem = pl.BlockSpec(memory_space=pltpu.SMEM)
    whole = lambda shape: pl.BlockSpec(shape, lambda g: (0,) * len(shape))
    cols = lambda part: pl.BlockSpec((WIDTH, HALF), lambda g: (0, 2 * part + g))
    return pl.pallas_call(
        partial(pack_kernel, cap),
        grid=(2,),
        in_specs=[
            smem,
            smem,
            smem,
            whole((2, ROWS, WIDTH)),
            whole((2, ROWS, WIDTH)),
            whole((1, WIDTH)),
            cols(0),
            cols(1),
            cols(2),
            pl.BlockSpec((HALF, WIDTH), lambda g: (g, 0)),
        ],
        out_specs=whole((HEADS, 3, cap, 128)),
        out_shape=jax.ShapeDtypeStruct((HEADS, 3, cap, 128), F32),
        scratch_shapes=[
            pltpu.VMEM((HEADS * 3, ROWS, 128), F32),
            pltpu.VMEM((4 * ROWS, WIDTH), BF16),
            pltpu.VMEM((4 * ROWS, WIDTH), BF16),
        ],
        compiler_params=pltpu.CompilerParams(vmem_limit_bytes=VMEM_LIMIT),
        name="project_pack",
    )(levels, offs, counts, x, cot, gain, w_qkv, w_qkv, w_qkv, w_out)


def attend(a, b, block):
    n = a.shape[1]
    q, k = a[:48] * SCALE, a[48:96]
    v = jnp.concatenate([a[96:128], b[:16]], axis=0)
    do = b[16:64]
    qh, ql = split(q)
    kh, kl = split(k)
    vh, vl = split(v)
    dh, dl = split(do)
    pad = jnp.zeros((80, n), F32)
    padh = jnp.zeros((80, n), BF16)
    q3 = jnp.concatenate([qh, qh, ql], axis=0).T
    d3 = jnp.concatenate([dh, dh, dl], axis=0).T
    k3 = jnp.concatenate([kh, kl, kh], axis=0)
    v3 = jnp.concatenate([vh, vl, vh], axis=0)
    v2 = jnp.concatenate([vh, padh, vl, padh], axis=0).T
    k2 = jnp.concatenate([kh, padh, kl, padh], axis=0).T
    do_t = jnp.concatenate([do, pad], axis=0).T
    q2 = jnp.concatenate([qh, ql], axis=0)
    d2 = jnp.concatenate([dh, dl], axis=0)
    outs, dqs = [], []
    dv = jnp.zeros((48, n), F32)
    dk = jnp.zeros((48, n), F32)

    def right(ph, plo, m2):
        both = dot(ph, m2)
        return both[:, :128] + both[:, 128:] + dot(plo, m2[:, :128])

    def left(m2, mh, ph, plo):
        both = dot(m2, ph)
        return both[:48] + both[48:] + dot(mh, plo)

    for i in range(0, n, block):
        r = slice(i, i + block)
        scores = dot(q3[r], k3)
        expo = jnp.exp(scores - jnp.max(scores, axis=-1, keepdims=True))
        prob = expo * (1.0 / jnp.sum(expo, axis=-1, keepdims=True))
        ph, plo = split(prob)
        out = right(ph, plo, v2)
        delta = jnp.sum(out * do_t[r], axis=-1, keepdims=True)
        ds = prob * (dot(d3[r], v3) - delta)
        sh, slo = split(ds)
        outs.append(out)
        dqs.append(right(sh, slo, k2))
        dv = dv + left(d2[:, r], dh[:, r], ph, plo)
        dk = dk + left(q2[:, r], qh[:, r], sh, slo)
    out = jnp.concatenate(outs, axis=0).T[:48]
    dq = jnp.concatenate(dqs, axis=0).T[:48] * SCALE
    return jnp.concatenate([dq, dk, dv[:32]], axis=0), jnp.concatenate([dv[32:], out], axis=0)


def attend_kernel(cap, levels, offs, place, buf, out, xa, xb, ya, yb):
    me = place[0]

    def solve(n, block):
        a = xa[:n].T
        b = xb[:n].T
        return attend(a, b, block)

    def one(h, carry):
        level, off = levels[h], offs[h]
        dst = off // cap
        row = pl.multiple_of(off % cap, 8)
        for lev in range(LEVELS):
            n_rows = ROWS >> lev
            wide = n_rows > cap
            mine = (me == dst) | (me == dst + 1) if wide else me == dst
            per_slot = max(1, 4 >> lev)
            n_src = 4 << lev if lev < 2 else 16
            n = n_src * n_rows
            units = per_slot if wide else 2 * per_slot

            @pl.when((level == lev) & mine)
            def _():
                def unit(u, inner):
                    if wide:
                        src = pl.ds(u * n_src, n_src)
                        a = jnp.concatenate(
                            [buf[src, j].reshape(n_src * cap, 128) for j in (0, 2)], axis=0
                        )
                        b = buf[src, 1].reshape(n_src * cap, 128).T
                        ra, rb = attend(
                            a.T, jnp.concatenate([b[:64], b[64:]], axis=1), min(n, 256)
                        )
                        ra = ra.T
                        half = n // 2
                        out[src, 0] = ra[:half].reshape(n_src, cap, 128)
                        out[src, 2] = ra[half:].reshape(n_src, cap, 128)
                        rb = jnp.concatenate([rb[:, :half], rb[:, half:]], axis=0).T
                        out[src, 1] = rb.reshape(n_src, cap, 128)
                    else:
                        slot, seg = u // per_slot, u % per_slot
                        src = pl.ds(seg * n_src, n_src)
                        rows = pl.ds(row, n_rows)
                        a = buf[src, 2 * slot, rows, :].reshape(n, 128).T
                        b = buf[src, 1, rows, :].reshape(n, 128).T
                        b = jnp.where(slot == 0, b[:64], b[64:])
                        ra, rb = attend(a, b, min(n, 256))
                        out[src, 2 * slot, rows, :] = ra.T.reshape(n_src, n_rows, 128)
                        rb = jnp.concatenate([rb, rb], axis=0).T.reshape(n_src, n_rows, 128)
                        old = out[src, 1, rows, :]
                        lane = lax.broadcasted_iota(jnp.int32, rb.shape, 2)
                        out[src, 1, rows, :] = jnp.where((lane >= 64) == (slot == 1), rb, old)
                    return inner

                lax.fori_loop(0, units, unit, 0)

        return carry

    lax.fori_loop(0, HEADS, one, 0)


def attention(cap, levels, offs, place, buf):
    smem = pl.BlockSpec(memory_space=pltpu.SMEM)
    vmem = pl.BlockSpec(memory_space=pltpu.VMEM)
    return pl.pallas_call(
        partial(attend_kernel, cap),
        in_specs=[smem, smem, smem, vmem],
        out_specs=vmem,
        out_shape=jax.ShapeDtypeStruct((HEADS, 3, cap, 128), F32),
        scratch_shapes=[pltpu.VMEM((8, 128), F32)] * 4,
        compiler_params=pltpu.CompilerParams(vmem_limit_bytes=VMEM_LIMIT),
        name="attention",
    )(levels, offs, place, buf)


def finish_kernel(
    cap, levels, offs, counts, place, buf, x, cot, gain, w_qkv, w_out,
    branch, input_grad, grad_gain, keep, send, tiles,
):
    core = place[0] % 2
    tiles[...] = jnp.zeros_like(tiles)

    def one(h, carry):
        level, off = levels[h], offs[h]
        for lev in range(LEVELS):
            n, rate = ROWS >> lev, 1 << lev

            @pl.when(level == lev)
            def _():
                dst = off // cap
                if n > cap:
                    pick = left_lanes((cap, 128))
                    for s in range(2):
                        tiles[h * 3 + 2 * s, pl.ds(0, cap), :] = buf[dst + s, 0]
                        tiles[h * 3 + 2 * s, pl.ds(cap, cap), :] = buf[dst + s, 2]
                    b0, b1 = buf[dst, 1], buf[dst + 1, 1]
                    tiles[h * 3 + 1, pl.ds(0, cap), :] = jnp.where(pick, b0, roll_half(b1))
                    tiles[h * 3 + 1, pl.ds(cap, cap), :] = jnp.where(pick, roll_half(b0), b1)
                else:
                    row = pl.multiple_of(off % cap, 8)
                    first = h % rate
                    for j in range(3):
                        to = pl.ds(first, n, stride=rate) if rate > 1 else pl.ds(0, n)
                        tiles[h * 3 + j, to, :] = buf[dst, j, pl.ds(row, n), :]

        return carry

    lax.fori_loop(0, HEADS, one, 0)

    live = live_rows(counts)
    xhat, rstd = normalise(x[...].reshape(2 * ROWS, WIDTH))
    n2 = stack(xhat * gain[...])
    masked = cot[...].reshape(2 * ROWS, WIDTH) * live

    def piece(h, s, which):
        wide, tail = tiles[h * 3 + 2 * s], tiles[h * 3 + 1]
        tail = tail[:, 64 * s : 64 * (s + 1)]
        if which == 0:
            return wide[:, :48]
        if which == 1:
            return wide[:, 48:96]
        if which == 2:
            return jnp.concatenate([wide[:, 96:], tail[:, :16]], axis=1)
        return tail[:, 16:]

    def columns(g, which):
        return jnp.concatenate(
            [
                jnp.concatenate([piece(g * 8 + i, s, which) for i in range(8)], axis=1)
                for s in range(2)
            ],
            axis=0,
        )

    def place_rows(value, index, row):
        z, xh, c = index // 4, index // 2 % 2, index % 2

        @pl.when(core == c)
        def _():
            keep[z, xh, row : row + HDIM] = value

        @pl.when(core != c)
        def _():
            send[z, xh, row : row + HDIM] = value

    def weight_grad(left, right2):
        lt = stack(left.T)
        m = left.shape[1]
        both = dot(lt, right2[: 2 * ROWS])
        return both[:m] + both[m:] + dot(lt[:m], right2[2 * ROWS :])

    dnormed = jnp.zeros((2 * ROWS, WIDTH), F32)
    for part in range(3):
        for g in range(2):
            value = columns(g, part)
            at = part * WIDTH + g * HALF
            grad = weight_grad(value, n2)
            for i in range(8):
                index = (part * 2 + g) * 8 + i
                place_rows(grad[HDIM * i : HDIM * (i + 1)], index // 3, HDIM * (index % 3))
            dnormed = dnormed + dot_stack(stack(value), w_qkv[:, at : at + HALF], ((1,), (1,)))
    attended2 = stack(jnp.concatenate([columns(0, 3), columns(1, 3)], axis=1))
    branch[...] = (dot_stack(attended2, w_out[...]) * live).reshape(2, ROWS, WIDTH)
    for g in range(2):
        grad = weight_grad(masked[:, g * HALF : (g + 1) * HALF], attended2)
        for i in range(8):
            place_rows(grad[HDIM * i : HDIM * (i + 1)], g * 8 + i, 3 * HDIM)
    grad_gain[...] = jnp.broadcast_to(jnp.sum(dnormed * xhat, axis=0, keepdims=True), (8, WIDTH))
    dxhat = dnormed * gain[...]
    mean_a = jnp.mean(dxhat, axis=-1, keepdims=True)
    mean_b = jnp.mean(dxhat * xhat, axis=-1, keepdims=True)
    input_grad[...] = (rstd * (dxhat - mean_a - xhat * mean_b)).reshape(2, ROWS, WIDTH)


def finish(cap, levels, offs, counts, place, buf, x, cot, gain, w_qkv, w_out):
    smem = pl.BlockSpec(memory_space=pltpu.SMEM)
    vmem = pl.BlockSpec(memory_space=pltpu.VMEM)
    return pl.pallas_call(
        partial(finish_kernel, cap),
        in_specs=[smem] * 4 + [vmem] * 6,
        out_specs=[vmem] * 5,
        out_shape=[
            jax.ShapeDtypeStruct((2, ROWS, WIDTH), F32),
            jax.ShapeDtypeStruct((2, ROWS, WIDTH), F32),
            jax.ShapeDtypeStruct((8, WIDTH), F32),
            jax.ShapeDtypeStruct((4, 2, 4 * HDIM, WIDTH), F32),
            jax.ShapeDtypeStruct((4, 2, 4 * HDIM, WIDTH), F32),
        ],
        scratch_shapes=[pltpu.VMEM((HEADS * 3, ROWS, 128), F32)],
        compiler_params=pltpu.CompilerParams(vmem_limit_bytes=VMEM_LIMIT),
        name="finish",
    )(levels, offs, counts, place, buf, x, cot, gain, w_qkv, w_out)


def seq_move(x, step):
    pairs = []
    for i in range(HEADS):
        z, xh, c = step(i // 4, i // 2 % 2, i % 2)
        pairs.append((i, (z % 4) * 4 + xh * 2 + c))
    return lax.ppermute(x, "seq", pairs)


def dp_move(x, step):
    pairs = []
    for i in range(8):
        y, xl = step(i // 2, i % 2)
        pairs.append((i, (y % 4) * 2 + xl))
    return lax.ppermute(x, "dp", pairs)


def both_move(x, step):
    pairs = []
    for d in range(8):
        for s in range(HEADS):
            xh, xl = step(s // 2 % 2, d % 2)
            pairs.append((d * HEADS + s, (d // 2 * 2 + xl) * HEADS + s // 4 * 4 + xh * 2 + s % 2))
    return lax.ppermute(x, ("dp", "seq"), pairs)


def pick(x, index, axis, size=1):
    return lax.dynamic_slice_in_dim(x, index, size, axis)


def reduce_all(keep, send, gain):
    place = lax.axis_index("seq")
    z, xh = place // 4, place // 2 % 2
    y = lax.axis_index("dp") // 2
    rows = 4 * HDIM
    half = rows // 2
    quarter = half // 4

    def join(body, extra):
        return jnp.concatenate([body.reshape(-1, WIDTH), extra], axis=0)

    got = seq_move(send, lambda z, xh, c: (z, xh, 1 - c))
    gain_got = seq_move(gain, lambda z, xh, c: (z, xh, 1 - c))
    total = keep + got
    gain = gain + gain_got

    zs, ys = total[:, :, :half], total[:, :, half:]
    zmsg = lambda k: pick(zs, (z + k) % 4, 0)
    ymsg = lambda k: pick(ys, ((y + k) % 4) * quarter, 2, quarter)
    z_in = [
        seq_move(join(zmsg(k), gain), lambda z, xh, c, k=k: (z + k, xh, c)) for k in (1, 2, 3)
    ]
    y_in = [dp_move(ymsg(k), lambda y, xl, k=k: (y + k, xl)) for k in (1, 2, 3)]
    z_sum = join(zmsg(0), gain) + z_in[0] + z_in[1] + z_in[2]
    y_sum = ymsg(0) + y_in[0] + y_in[1] + y_in[2]
    gain = z_sum[2 * half :]
    zs = z_sum[: 2 * half].reshape(2, half, WIDTH)

    zmsg = lambda k: pick(zs, ((y + k) % 4) * quarter, 1, quarter)
    ymsg = lambda k: pick(y_sum, (z + k) % 4, 0)
    z_in = [dp_move(join(zmsg(k), gain), lambda y, xl, k=k: (y + k, xl)) for k in (1, 2, 3)]
    y_in = [seq_move(ymsg(k), lambda z, xh, c, k=k: (z + k, xh, c)) for k in (1, 2, 3)]
    z_sum = join(zmsg(0), gain) + z_in[0] + z_in[1] + z_in[2]
    y_sum = ymsg(0) + y_in[0] + y_in[1] + y_in[2]
    gain = z_sum[2 * quarter :]
    both = jnp.concatenate([z_sum[: 2 * quarter].reshape(2, quarter, WIDTH), y_sum[0]], axis=1)

    own = join(pick(both, xh, 0), gain)
    other = join(pick(both, 1 - xh, 0), gain)
    x_in = [
        both_move(own, lambda xh, xl: (xh, 1 - xl)),
        both_move(other, lambda xh, xl: (1 - xh, xl)),
        both_move(other, lambda xh, xl: (1 - xh, 1 - xl)),
    ]
    mine = own + x_in[0] + x_in[1] + x_in[2]
    body, gain = mine[: 2 * quarter], mine[2 * quarter]

    pieces = [body] + [dp_move(body, lambda y, xl, k=k: (y + k, xl)) for k in (1, 2, 3)]
    pieces = jnp.stack(pieces)
    order = [pick(pieces, (y - i) % 4, 0)[0] for i in range(4)]
    full = jnp.concatenate(
        [o[:quarter] for o in order] + [o[quarter:] for o in order], axis=0
    )
    gain = lax.dynamic_slice_in_dim(gain, place * HDIM, HDIM)
    return gain, full[: 3 * HDIM].T, full[3 * HDIM :].T


def shards(slides, counts, levels, norm_gain, w_qkv, w_out, cotangent):
    x, cot = slides[0], cotangent[0]
    place = lax.axis_index("seq")[None]
    gain = norm_gain[None]
    sizes = ROWS >> levels
    ids = jnp.arange(HEADS, dtype=jnp.int32)
    before = (levels[None] < levels[:, None]) | (
        (levels[None] == levels[:, None]) & (ids[None] < ids[:, None])
    )
    offs = jnp.sum(jnp.where(before, sizes[None], 0), axis=1, dtype=jnp.int32)

    def run(cap, x, cot):
        packed = pack(cap, levels, offs, counts, x, cot, gain, w_qkv, w_out)
        packed = lax.all_to_all(packed, "seq", split_axis=0, concat_axis=0, tiled=True)
        result = attention(cap, levels, offs, place, packed)
        result = lax.all_to_all(result, "seq", split_axis=0, concat_axis=0, tiled=True)
        return finish(cap, levels, offs, counts, place, result, x, cot, gain, w_qkv, w_out)

    branch, input_grad, gain_part, keep, send = lax.cond(
        jnp.sum(sizes) <= HEADS * ROWS // 2, partial(run, ROWS // 2), partial(run, ROWS), x, cot
    )
    grad_gain, grad_qkv, grad_out = reduce_all(keep, send, gain_part)
    return branch[None], input_grad[None], grad_gain, grad_qkv, grad_out


def solution(mesh):
    return jax.shard_map(
        shards,
        mesh=mesh,
        in_specs=(
            P("dp", None, "seq", None),
            P("dp"),
            P(),
            P(),
            P(),
            P(),
            P("dp", None, "seq", None),
        ),
        out_specs=(
            P("dp", None, "seq", None),
            P("dp", None, "seq", None),
            P("seq"),
            P(None, "seq"),
            P(None, "seq"),
        ),
        check_vma=False,
    )
```

```python
from functools import partial

import jax
import jax.numpy as jnp
from jax import lax
from jax.experimental import pallas as pl
from jax.experimental.pallas import tpu as pltpu
from jax.sharding import PartitionSpec as P

HEADS = 16
HDIM = 48
LEVELS = 5
EPS = 1e-05
ROWS = 128
CAP = 64
BLOCK = 256
WIDTH = 768
SCALE = HDIM**-0.5
F32 = jnp.float32
BF16 = jnp.bfloat16
VMEM_LIMIT = 60 * 1024 * 1024


def split(x):
    hi = x.astype(BF16)
    return hi, (x - hi.astype(F32)).astype(BF16)


def dot(a, b, dims=((1,), (0,))):
    return lax.dot_general(a, b, (dims, ((), ())), preferred_element_type=F32)


def dot_stack(a2, w, dims=((1,), (0,))):
    m = a2.shape[0] // 2
    wh, wl = split(w)
    both = dot(a2, wh, dims)
    return both[:m] + both[m:] + dot(a2[:m], wl, dims)


def stack(x):
    return jnp.concatenate(split(x), axis=0)


def normalise(x):
    mean = jnp.mean(x, axis=-1, keepdims=True)
    centred = x - mean
    rstd = lax.rsqrt(jnp.mean(centred * centred, axis=-1, keepdims=True) + EPS)
    return centred * rstd, rstd


def live_rows(counts):
    rows = lax.broadcasted_iota(jnp.int32, (2 * ROWS, 1), 0)
    return (rows < counts[0] * ROWS).astype(F32)


def roll_half(x):
    return pltpu.roll(x, 64, 1)


def left_lanes(shape):
    return lax.broadcasted_iota(jnp.int32, shape, 1) < 64


def pack_kernel(levels, counts, x, cot, gain, wqkv, wo, out0, out1, offs, full, tiles, n2, c2, bins):
    g = pl.program_id(0)

    @pl.when(g == 0)
    def _():
        xhat, _ = normalise(x[...].reshape(2 * ROWS, WIDTH))
        n2[...] = stack(xhat * gain[...][None])
        c2[...] = stack(cot[...].reshape(2 * ROWS, WIDTH) * live_rows(counts))
        at = jnp.int32(0)
        for lev in range(LEVELS):
            for h in range(HEADS):
                here = levels[h] == lev

                @pl.when(here)
                def _():
                    offs[h] = at

                at = at + jnp.where(here, ROWS >> lev, 0)
        full[0] = (at > HEADS * CAP).astype(jnp.int32)
        do = dot_stack(c2[...], wo[...], ((1,), (1,)))
        for h in range(HEADS):
            for s in range(2):
                piece = do[ROWS * s : ROWS * (s + 1), HDIM * h : HDIM * (h + 1)]
                tiles[h * 3 + 1, :, 64 * s + 16 : 64 * (s + 1)] = piece

    for part in range(3):

        @pl.when(g == part + 1)
        def _():
            value = dot_stack(n2[...], wqkv[...])
            for h in range(HEADS):
                for s in range(2):
                    piece = value[ROWS * s : ROWS * (s + 1), HDIM * h : HDIM * (h + 1)]
                    if part < 2:
                        tiles[h * 3 + 2 * s, :, HDIM * part : HDIM * (part + 1)] = piece
                    else:
                        tiles[h * 3 + 2 * s, :, 96:] = piece[:, :32]
                        tiles[h * 3 + 1, :, 64 * s : 64 * s + 16] = piece[:, 32:]

    @pl.when(g == 3)
    def _():
        def one(h, carry):
            level, off = levels[h], offs[h]
            b = off // CAP
            for lev in range(LEVELS):
                n, rate = ROWS >> lev, 1 << lev

                @pl.when(level == lev)
                def _():
                    if n > CAP:
                        t = tiles[h * 3 + 1]
                        top, low = t[:CAP], t[CAP:]
                        pick = left_lanes(top.shape)
                        for s in range(2):
                            bins[b + s, 0] = tiles[h * 3 + 2 * s, :CAP, :]
                            bins[b + s, 2] = tiles[h * 3 + 2 * s, CAP:, :]
                        bins[b, 1] = jnp.where(pick, top, roll_half(low))
                        bins[b + 1, 1] = jnp.where(pick, roll_half(top), low)
                    else:
                        row = pl.multiple_of(off % CAP, 8)
                        first = h % rate
                        for j in range(3):
                            src = pl.ds(first, n, stride=rate)
                            bins[b, j, pl.ds(row, n), :] = tiles[h * 3 + j, src, :]

            return carry

        lax.fori_loop(0, HEADS, one, 0)
        out0[...] = bins[:HEADS]

        @pl.when(full[0] > 0)
        def _():
            out1[...] = bins[HEADS:]


def smem_spec():
    return pl.BlockSpec(memory_space=pltpu.SMEM)


def vmem_spec():
    return pl.BlockSpec(memory_space=pltpu.VMEM)


BINS = jax.ShapeDtypeStruct((HEADS, 3, CAP, 128), F32)


def pack(levels, counts, x, cot, gain, w_qkv, w_out):
    whole = lambda shape: pl.BlockSpec(shape, lambda g: (0,) * len(shape))
    return pl.pallas_call(
        pack_kernel,
        grid=(4,),
        in_specs=[
            smem_spec(),
            smem_spec(),
            whole((2, ROWS, WIDTH)),
            whole((2, ROWS, WIDTH)),
            whole((WIDTH,)),
            pl.BlockSpec((WIDTH, WIDTH), lambda g: (0, jnp.maximum(g - 1, 0))),
            whole((WIDTH, WIDTH)),
        ],
        out_specs=[whole(BINS.shape), whole(BINS.shape), smem_spec(), smem_spec()],
        out_shape=[
            BINS,
            BINS,
            jax.ShapeDtypeStruct((HEADS,), jnp.int32),
            jax.ShapeDtypeStruct((1,), jnp.int32),
        ],
        scratch_shapes=[
            pltpu.VMEM((HEADS * 3, ROWS, 128), F32),
            pltpu.VMEM((4 * ROWS, WIDTH), BF16),
            pltpu.VMEM((4 * ROWS, WIDTH), BF16),
            pltpu.VMEM((2 * HEADS, 3, CAP, 128), F32),
        ],
        compiler_params=pltpu.CompilerParams(vmem_limit_bytes=VMEM_LIMIT),
        cost_estimate=pl.CostEstimate(
            flops=6 * 256 * 768 * 3072, bytes_accessed=14_000_000, transcendentals=0
        ),
        name="project_pack",
    )(levels, counts, x, cot, gain, w_qkv, w_out)


def attend(a, b, block):
    n = a.shape[1]
    q, k = a[:48] * SCALE, a[48:96]
    v = jnp.concatenate([a[96:128], b[:16]], axis=0)
    do = b[16:64]
    qh, ql = split(q)
    kh, kl = split(k)
    vh, vl = split(v)
    dh, dl = split(do)
    pad = jnp.zeros((80, n), F32)
    padh = jnp.zeros((80, n), BF16)
    q3 = jnp.concatenate([qh, qh, ql], axis=0).T
    d3 = jnp.concatenate([dh, dh, dl], axis=0).T
    k3 = jnp.concatenate([kh, kl, kh], axis=0)
    v3 = jnp.concatenate([vh, vl, vh], axis=0)
    v2 = jnp.concatenate([vh, padh, vl, padh], axis=0).T
    k2 = jnp.concatenate([kh, padh, kl, padh], axis=0).T
    do_t = jnp.concatenate([do, pad], axis=0).T
    q2 = jnp.concatenate([qh, ql], axis=0)
    d2 = jnp.concatenate([dh, dl], axis=0)
    outs, dqs = [], []
    dv = jnp.zeros((48, n), F32)
    dk = jnp.zeros((48, n), F32)

    def right(ph, plo, m2):
        both = dot(ph, m2)
        return both[:, :128] + both[:, 128:] + dot(plo, m2[:, :128])

    def left(m2, mh, ph, plo):
        both = dot(m2, ph)
        return both[:48] + both[48:] + dot(mh, plo)

    for i in range(0, n, block):
        r = slice(i, i + block)
        scores = dot(q3[r], k3)
        expo = jnp.exp(scores - jnp.max(scores, axis=-1, keepdims=True))
        prob = expo * (1.0 / jnp.sum(expo, axis=-1, keepdims=True))
        ph, plo = split(prob)
        out = right(ph, plo, v2)
        delta = jnp.sum(out * do_t[r], axis=-1, keepdims=True)
        ds = prob * (dot(d3[r], v3) - delta)
        sh, slo = split(ds)
        outs.append(out)
        dqs.append(right(sh, slo, k2))
        dv = dv + left(d2[:, r], dh[:, r], ph, plo)
        dk = dk + left(q2[:, r], qh[:, r], sh, slo)
    out = jnp.concatenate(outs, axis=0).T[:48]
    dq = jnp.concatenate(dqs, axis=0).T[:48] * SCALE
    return jnp.concatenate([dq, dk, dv[:32]], axis=0), jnp.concatenate([dv[32:], out], axis=0)


def attend_kernel(levels, offs, place, in0, in1, out0, out1):
    me = place[0]

    def one(h, carry):
        level, off = levels[h], offs[h]
        b = off // CAP
        for lev in range(LEVELS):
            n_rows = ROWS >> lev
            wide = n_rows > CAP
            per_slot = max(1, 4 >> lev)
            n_src = 4 << lev if lev < 2 else 16
            n = n_src * n_rows
            half = n // 2
            if wide:
                mine = ((b % HEADS) == me) | (((b + 1) % HEADS) == me)
                plane = jnp.where((b % HEADS) == me, b, b + 1) // HEADS
            else:
                mine = (b % HEADS) == me
                plane = b // HEADS

            @pl.when((level == lev) & mine)
            def _():
                def load(*at):
                    return jnp.where(plane == 0, in0[at], in1[at])

                def store(value, *at):
                    @pl.when(plane == 0)
                    def _():
                        out0[at] = value

                    @pl.when(plane != 0)
                    def _():
                        out1[at] = value

                def unit(u, inner):
                    if wide:
                        src = pl.ds(u * n_src, n_src)
                        a = [load(src, j).reshape(half, 128) for j in (0, 2)]
                        t = load(src, 1).reshape(half, 128).T
                        ra, rb = attend(
                            jnp.concatenate(a, axis=0).T,
                            jnp.concatenate([t[:64], t[64:]], axis=1),
                            min(n, BLOCK),
                        )
                        ra = ra.T
                        rb = jnp.concatenate([rb[:, :half], rb[:, half:]], axis=0).T
                        store(ra[:half].reshape(n_src, CAP, 128), src, 0)
                        store(ra[half:].reshape(n_src, CAP, 128), src, 2)
                        store(rb.reshape(n_src, CAP, 128), src, 1)
                    else:
                        row = pl.multiple_of(off % CAP, 8)
                        slot, seg = u // per_slot, u % per_slot
                        src = pl.ds(seg * n_src, n_src)
                        rows = pl.ds(row, n_rows)
                        a = load(src, 2 * slot, rows, slice(None)).reshape(n, 128).T
                        t = load(src, 1, rows, slice(None)).reshape(n, 128).T
                        t = jnp.where(slot == 0, t[:64], t[64:])
                        ra, rb = attend(a, t, min(n, BLOCK))
                        store(ra.T.reshape(n_src, n_rows, 128), src, 2 * slot, rows, slice(None))
                        rb = jnp.concatenate([rb, rb], axis=0).T.reshape(n_src, n_rows, 128)
                        old = jnp.where(plane == 0, out0[src, 1, rows, :], out1[src, 1, rows, :])
                        lane = lax.broadcasted_iota(jnp.int32, rb.shape, 2)
                        rb = jnp.where((lane >= 64) == (slot == 1), rb, old)
                        store(rb, src, 1, rows, slice(None))
                    return inner

                lax.fori_loop(0, per_slot if wide else 2 * per_slot, unit, 0)

        return carry

    lax.fori_loop(0, HEADS, one, 0)


def attention(levels, offs, place, in0, in1):
    return pl.pallas_call(
        attend_kernel,
        in_specs=[smem_spec()] * 3 + [vmem_spec()] * 2,
        out_specs=[vmem_spec()] * 2,
        out_shape=[BINS, BINS],
        compiler_params=pltpu.CompilerParams(vmem_limit_bytes=VMEM_LIMIT),
        cost_estimate=pl.CostEstimate(
            flops=10_000_000_000, bytes_accessed=6_000_000, transcendentals=1_000_000
        ),
        name="attention",
    )(levels, offs, place, in0, in1)


def unpack(levels, offs, in0, in1, tiles):
    tiles[...] = jnp.zeros_like(tiles)

    def one(h, carry):
        level, off = levels[h], offs[h]
        b = off // CAP

        def load(b, *at):
            dev = b % HEADS
            return jnp.where(b < HEADS, in0[(dev, *at)], in1[(dev, *at)])

        for lev in range(LEVELS):
            n, rate = ROWS >> lev, 1 << lev

            @pl.when(level == lev)
            def _():
                if n > CAP:
                    pick = left_lanes((CAP, 128))
                    for s in range(2):
                        tiles[h * 3 + 2 * s, :CAP, :] = load(b + s, 0)
                        tiles[h * 3 + 2 * s, CAP:, :] = load(b + s, 2)
                    b0, b1 = load(b, 1), load(b + 1, 1)
                    tiles[h * 3 + 1, :CAP, :] = jnp.where(pick, b0, roll_half(b1))
                    tiles[h * 3 + 1, CAP:, :] = jnp.where(pick, roll_half(b0), b1)
                else:
                    row = pl.multiple_of(off % CAP, 8)
                    for j in range(3):
                        to = pl.ds(h % rate, n, stride=rate)
                        tiles[h * 3 + j, to, :] = load(b, j, pl.ds(row, n), slice(None))

        return carry

    lax.fori_loop(0, HEADS, one, 0)


def head_piece(tiles, h, s, which):
    if which < 2:
        return tiles[h * 3 + 2 * s][:, HDIM * which : HDIM * (which + 1)]
    tail = tiles[h * 3 + 1][:, 64 * s : 64 * (s + 1)]
    if which == 2:
        return jnp.concatenate([tiles[h * 3 + 2 * s][:, 96:], tail[:, :16]], axis=1)
    return tail[:, 16:]


def columns(tiles, pairs):
    return jnp.concatenate(
        [
            jnp.concatenate([head_piece(tiles, h, s, which) for which, h in pairs], axis=1)
            for s in range(2)
        ],
        axis=0,
    )


def prepare_kernel(counts, place, xa, xb, ca, cb, gain, n2, m2):
    core = place[0] % 2
    live = live_rows(counts)
    for t, (x, cot) in enumerate(((xa, ca), (xb, cb))):
        tok = slice(2 * ROWS * t, 2 * ROWS * (t + 1))
        xhat, _ = normalise(x[...].reshape(2 * ROWS, WIDTH))
        for part, value in enumerate(split(xhat * gain[...][None])):
            n2[part, tok] = value
        masked = cot[...].reshape(2 * ROWS, WIDTH) * live
        for c in range(2):

            @pl.when(core == c)
            def _():
                mine = [masked[:, HDIM * (2 * j + c) : HDIM * (2 * j + c + 1)] for j in range(8)]
                for part, value in enumerate(split(jnp.concatenate(mine, axis=1).T)):
                    m2[part, :, tok] = value


def prepare(counts, place, xa, xb, ca, cb, gain):
    return pl.pallas_call(
        prepare_kernel,
        in_specs=[smem_spec()] * 2 + [vmem_spec()] * 5,
        out_specs=[vmem_spec()] * 2,
        out_shape=[
            jax.ShapeDtypeStruct((2, 4 * ROWS, WIDTH), BF16),
            jax.ShapeDtypeStruct((2, WIDTH // 2, 4 * ROWS), BF16),
        ],
        compiler_params=pltpu.CompilerParams(vmem_limit_bytes=VMEM_LIMIT),
        cost_estimate=pl.CostEstimate(
            flops=2_000_000_000, bytes_accessed=6_000_000, transcendentals=0
        ),
        name="prepare",
    )(counts, place, xa, xb, ca, cb, gain)


def grad_kernel(
    levels, offs, place, a0, a1, b0, b1, n2, m2,
    z_own, z_up, z_down, z_right, z_left, y_own, y_up, y_down, y_right, y_left,
    tiles, left, o2, rows,
):
    core, z_me, y_me = place[0] % 2, place[0] // 4, place[1]
    for t, (in0, in1) in enumerate(((a0, a1), (b0, b1))):
        tok = slice(2 * ROWS * t, 2 * ROWS * (t + 1))
        unpack(levels, offs, in0, in1, tiles)
        attended = columns(tiles, [(3, h) for h in range(HEADS)])
        for part, value in enumerate(split(attended)):
            o2[part, tok] = value
        for c in range(2):

            @pl.when(core == c)
            def _():
                for j in range(0, 8, 2):
                    at = [3 * (2 * (j + i // 3) + c) + i % 3 for i in range(6)]
                    value = columns(tiles, [(p // HEADS, p % HEADS) for p in at])
                    for part, piece in enumerate(split(value.T)):
                        left[part, 144 * j : 144 * (j + 2), tok] = piece

    for i in range(0, WIDTH, 256):
        cols = slice(i, i + 256)
        nh, nl = n2[0, :, cols], n2[1, :, cols]
        grad = dot(left[0], nh) + dot(left[1], nh) + dot(left[0], nl)
        oh, ol = o2[0, :, cols], o2[1, :, cols]
        out = dot(m2[0], oh) + dot(m2[1], oh) + dot(m2[0], ol)
        for j in range(8):
            rows[j, :144, cols] = grad[144 * j : 144 * (j + 1)]
            rows[j, 144:, cols] = out[HDIM * j : HDIM * (j + 1)]

    def z_part(k, xh):
        return rows[(z_me + k) % 4 * 2 + xh, :96, :]

    for xh in range(2):
        z_own[xh] = z_part(0, xh)
    z_up[0], z_up[1] = z_part(2, 0), z_part(1, 1)
    z_down[0], z_down[1] = z_part(3, 0), z_part(2, 1)
    z_right[...], z_left[...] = z_part(1, 0), z_part(3, 1)

    def y_part(k, z, xh):
        at = pl.multiple_of(96 + 24 * ((y_me + k) % 4), 8)
        return rows[z * 2 + xh, pl.ds(at, 24), :]

    for xh in range(2):
        for z in range(4):
            y_own[z, xh] = y_part(0, z, xh)
        for z in range(2):
            y_up[0, z, xh], y_up[1, z, xh] = y_part(2, z, xh), y_part(1, z + 2, xh)
            y_down[0, z, xh], y_down[1, z, xh] = y_part(3, z, xh), y_part(2, z + 2, xh)
            y_right[z, xh], y_left[z, xh] = y_part(1, z, xh), y_part(3, z + 2, xh)


def grads(levels, offs, place, a0, a1, b0, b1, n2, m2):
    zh, yh = (96, WIDTH), (2, 2, 24, WIDTH)
    shapes = [(2, *zh)] * 3 + [zh] * 2 + [(4, *yh[1:])] + [(2, *yh)] * 2 + [yh] * 2
    return pl.pallas_call(
        grad_kernel,
        in_specs=[smem_spec()] * 3 + [vmem_spec()] * 6,
        out_specs=[vmem_spec()] * 10,
        out_shape=[jax.ShapeDtypeStruct(shape, F32) for shape in shapes],
        scratch_shapes=[
            pltpu.VMEM((HEADS * 3, ROWS, 128), F32),
            pltpu.VMEM((2, 8 * 144, 4 * ROWS), BF16),
            pltpu.VMEM((2, 4 * ROWS, WIDTH), BF16),
            pltpu.VMEM((8, 192, WIDTH), F32),
        ],
        compiler_params=pltpu.CompilerParams(vmem_limit_bytes=VMEM_LIMIT),
        cost_estimate=pl.CostEstimate(
            flops=6 * 256 * 768 * 3072, bytes_accessed=14_000_000, transcendentals=0
        ),
        name="weight_grads",
    )(levels, offs, place, a0, a1, b0, b1, n2, m2)


def outputs_kernel(
    levels, offs, counts, in0, in1, x, gain, w_qkv, w_out, branch, input_grad, grad_gain, tiles
):
    unpack(levels, offs, in0, in1, tiles)
    live = live_rows(counts)
    xhat, rstd = normalise(x[...].reshape(2 * ROWS, WIDTH))
    dnormed = jnp.zeros((2 * ROWS, WIDTH), F32)
    for part in range(3):
        value = stack(columns(tiles, [(part, h) for h in range(HEADS)]))
        at = part * WIDTH
        dnormed = dnormed + dot_stack(value, w_qkv[:, at : at + WIDTH], ((1,), (1,)))
    attended2 = stack(columns(tiles, [(3, h) for h in range(HEADS)]))
    branch[...] = (dot_stack(attended2, w_out[...]) * live).reshape(2, ROWS, WIDTH)
    grad_gain[...] = jnp.sum(dnormed * xhat, axis=0)
    dxhat = dnormed * gain[...][None]
    mean_a = jnp.mean(dxhat, axis=-1, keepdims=True)
    mean_b = jnp.mean(dxhat * xhat, axis=-1, keepdims=True)
    input_grad[...] = (rstd * (dxhat - mean_a - xhat * mean_b)).reshape(2, ROWS, WIDTH)


def outputs(levels, offs, counts, in0, in1, x, gain, w_qkv, w_out):
    return pl.pallas_call(
        outputs_kernel,
        in_specs=[smem_spec()] * 3 + [vmem_spec()] * 6,
        out_specs=[vmem_spec()] * 3,
        out_shape=[
            jax.ShapeDtypeStruct((2, ROWS, WIDTH), F32),
            jax.ShapeDtypeStruct((2, ROWS, WIDTH), F32),
            jax.ShapeDtypeStruct((WIDTH,), F32),
        ],
        scratch_shapes=[pltpu.VMEM((HEADS * 3, ROWS, 128), F32)],
        compiler_params=pltpu.CompilerParams(vmem_limit_bytes=VMEM_LIMIT),
        cost_estimate=pl.CostEstimate(
            flops=6 * 256 * 768 * 3072, bytes_accessed=14_000_000, transcendentals=0
        ),
        name="outputs",
    )(levels, offs, counts, in0, in1, x, gain, w_qkv, w_out)


def seq_move(x, step):
    pairs = []
    for i in range(HEADS):
        z, xh, c = step(i // 4, i // 2 % 2, i % 2)
        pairs.append((i, (z % 4) * 4 + xh * 2 + c))
    return lax.ppermute(x, "seq", pairs)


def core_move(x):
    return seq_move(x, lambda z, xh, c: (z, xh, 1 - c))


def z_move(x, k):
    return seq_move(x, lambda z, xh, c: (z + k, xh, c))


def y_move(x, k):
    return lax.ppermute(x, "dp", [(i, (i // 2 + k) % 4 * 2 + i % 2) for i in range(8)])


def x_move(x, step):
    pairs = []
    for d in range(8):
        for s in range(HEADS):
            xh, xl = step(s // 2 % 2, d % 2)
            pairs.append((d * HEADS + s, (d // 2 * 2 + xl) * HEADS + s // 4 * 4 + xh * 2 + s % 2))
    return lax.ppermute(x, ("dp", "seq"), pairs)


def pick(x, index, axis, size=1):
    return lax.dynamic_slice_in_dim(x, index, size, axis)


def ring_send(move, up, down):
    return move(up, 1), move(down, -1)


def ring_sum(move, own, right, left, from_left, from_right):
    right = move(right + from_left[0], 1)
    left = move(left + from_right[1], -1)
    return own[0] + right + from_right[0], own[1] + from_left[1] + left


def reduce_all(parts, finish_outputs):
    place = lax.axis_index("seq")
    z, xh = place // 4, place // 2 % 2
    y = lax.axis_index("dp") // 2
    quarter = 24

    z_own, z_up, z_down, z_right, z_left, y_own, y_up, y_down, y_right, y_left = parts
    sent = ring_send(z_move, z_up, z_down), ring_send(y_move, y_up, y_down)
    done = finish_outputs()
    (z_in, y_in), done = lax.optimization_barrier((sent, done))
    branch, input_grad, gain = done
    zs = jnp.stack(ring_sum(z_move, z_own, z_right, z_left, *z_in))
    y_own = y_own.reshape(2, 2, *y_own.shape[1:])
    ys = jnp.concatenate(ring_sum(y_move, y_own, y_right, y_left, *y_in), axis=0)

    zmsg = lambda k: pick(zs, ((y + k) % 4) * quarter, 1, quarter)
    ymsg = lambda k: pick(ys, (z + k) % 4, 0)[0]
    z_sum, y_sum = zmsg(0), ymsg(0)
    for k in (1, 2, 3):
        z_sum = z_sum + y_move(zmsg(k), k)
        y_sum = y_sum + z_move(ymsg(k), k)
    both = jnp.concatenate([z_sum, y_sum], axis=1)

    gain, _ = lax.optimization_barrier((gain, zs))
    gain = lax.all_to_all(gain.reshape(HEADS, HDIM), "seq", split_axis=0, concat_axis=0, tiled=True)
    gain = jnp.sum(gain, axis=0)
    gain = jnp.broadcast_to(jnp.pad(gain, (0, WIDTH - HDIM)), (8, WIDTH))

    def join(body, extra):
        return jnp.concatenate([body.reshape(-1, WIDTH), extra], axis=0)

    own, other = join(pick(both, xh, 0), gain), pick(both, 1 - xh, 0)[0]
    mine = own + x_move(own, lambda xh, xl: (xh, 1 - xl))
    body = (
        mine[: 2 * quarter]
        + x_move(other, lambda xh, xl: (1 - xh, xl))
        + x_move(other, lambda xh, xl: (1 - xh, 1 - xl))
    )

    piece = join(body, mine[2 * quarter :])
    pieces = jnp.stack([piece] + [y_move(piece, k) for k in (1, 2, 3)])
    gain = jnp.sum(pieces[:, 2 * quarter, :HDIM], axis=0)
    order = [pick(pieces, (y - i) % 4, 0)[0] for i in range(4)]
    full = jnp.concatenate(
        [o[:quarter] for o in order] + [o[quarter : 2 * quarter] for o in order], axis=0
    )
    return branch, input_grad, gain, full[: 3 * HDIM].T, full[3 * HDIM :].T


def shards(slides, counts, levels, norm_gain, w_qkv, w_out, cotangent):
    x, cot = slides[0], cotangent[0]
    place = jnp.stack([lax.axis_index("seq"), lax.axis_index("dp") // 2])
    exchange = lambda v: lax.all_to_all(v, "seq", split_axis=0, concat_axis=0, tiled=True)
    x_b, cot_b = core_move(x), core_move(cot)
    sent0, sent1, offs, full = pack(levels, counts, x, cot, norm_gain, w_qkv, w_out)
    more = full[0] > 0
    got0 = exchange(sent0)
    got1 = lax.cond(more, exchange, lambda v: v, sent1)
    n2, m2 = prepare(counts, place, x, x_b, cot, cot_b, norm_gain)
    got0, n2, m2 = lax.optimization_barrier((got0, n2, m2))
    back0, back1 = attention(levels, offs, place, got0, got1)
    a0 = exchange(back0)
    b0 = core_move(a0)

    def second(v, unused):
        v = exchange(v)
        return v, core_move(v)

    a1, b1 = lax.cond(more, second, lambda v, unused: (v, unused), back1, got1)
    parts = grads(levels, offs, place, a0, a1, b0, b1, n2, m2)
    branch, input_grad, grad_gain, grad_qkv, grad_out = reduce_all(
        parts, lambda: outputs(levels, offs, counts, a0, a1, x, norm_gain, w_qkv, w_out)
    )
    return branch[None], input_grad[None], grad_gain, grad_qkv, grad_out


def solution(mesh):
    return jax.shard_map(
        shards,
        mesh=mesh,
        in_specs=(
            P("dp", None, "seq", None),
            P("dp"),
            P(),
            P(),
            P(),
            P(),
            P("dp", None, "seq", None),
        ),
        out_specs=(
            P("dp", None, "seq", None),
            P("dp", None, "seq", None),
            P("seq"),
            P(None, "seq"),
            P(None, "seq"),
        ),
        check_vma=False,
    )
```

```python
from functools import partial

import jax
import jax.numpy as jnp
from jax import lax
from jax.experimental import pallas as pl
from jax.experimental.pallas import tpu as pltpu
from jax.sharding import PartitionSpec as P

HEADS = 16
HDIM = 48
LEVELS = 5
EPS = 1e-05
ROWS = 128
CAP = 64
BLOCK = 512
WIDTH = 768
SCALE = HDIM**-0.5
F32 = jnp.float32
BF16 = jnp.bfloat16
MIB = 1024 * 1024


def split(x):
    hi = x.astype(BF16)
    return hi, (x - hi.astype(F32)).astype(BF16)


def dot(a, b, dims=((1,), (0,))):
    return lax.dot_general(a, b, (dims, ((), ())), preferred_element_type=F32)


def dot_stack(a2, w, dims=((1,), (0,))):
    m = a2.shape[0] // 2
    wh, wl = split(w)
    both = dot(a2, wh, dims)
    return both[:m] + both[m:] + dot(a2[:m], wl, dims)


def stack(x):
    return jnp.concatenate(split(x), axis=0)


def normalise(x):
    mean = jnp.mean(x, axis=-1, keepdims=True)
    centred = x - mean
    rstd = lax.rsqrt(jnp.mean(centred * centred, axis=-1, keepdims=True) + EPS)
    return centred * rstd, rstd


def live_rows(counts):
    rows = lax.broadcasted_iota(jnp.int32, (2 * ROWS, 1), 0)
    return (rows < counts[0] * ROWS).astype(F32)


def roll_half(x):
    return pltpu.roll(x, 64, 1)


def left_lanes(shape):
    return lax.broadcasted_iota(jnp.int32, shape, 1) < 64


def pack_kernel(
    levels, counts, x, far_cot, gain, wqkv, far_wo, out0, out1, offs, full,
    tiles, n2, bins, cot, wo, sems,
):
    g = pl.program_id(0)
    later = [
        pltpu.make_async_copy(far_cot, cot, sems.at[0]),
        pltpu.make_async_copy(far_wo, wo, sems.at[1]),
    ]

    @pl.when(g == 0)
    def _():
        for copy in later:
            copy.start()
        xhat, _ = normalise(x[...].reshape(2 * ROWS, WIDTH))
        n2[...] = stack(xhat * gain[...][None])
        heads = [levels[h] for h in range(HEADS)]
        at, firsts = jnp.int32(0), []
        for lev in range(LEVELS):
            firsts.append(at)
            for level in heads:
                at = at + jnp.where(level == lev, ROWS >> lev, 0)
        full[0] = (at > HEADS * CAP).astype(jnp.int32)
        for h, level in enumerate(heads):
            off = jnp.int32(0)
            for lev in range(LEVELS):
                here = level == lev
                off = jnp.where(here, firsts[lev], off)
                firsts[lev] = firsts[lev] + jnp.where(here, ROWS >> lev, 0)
            offs[h] = off

    for part in range(3):

        @pl.when(g == part)
        def _():
            value = dot_stack(n2[...], wqkv[...])
            for h in range(HEADS):
                for s in range(2):
                    piece = value[ROWS * s : ROWS * (s + 1), HDIM * h : HDIM * (h + 1)]
                    if part < 2:
                        tiles[h * 3 + 2 * s, :, HDIM * part : HDIM * (part + 1)] = piece
                    else:
                        tiles[h * 3 + 2 * s, :, 96:] = piece[:, :32]
                        tiles[h * 3 + 1, :, 64 * s : 64 * s + 16] = piece[:, 32:]

    @pl.when(g == 2)
    def _():
        for copy in later:
            copy.wait()
        c2 = stack(cot[...].reshape(2 * ROWS, WIDTH) * live_rows(counts))
        do = dot_stack(c2, wo[...], ((1,), (1,)))
        for h in range(HEADS):
            for s in range(2):
                piece = do[ROWS * s : ROWS * (s + 1), HDIM * h : HDIM * (h + 1)]
                tiles[h * 3 + 1, :, 64 * s + 16 : 64 * (s + 1)] = piece

        def one(h, carry):
            level, off = levels[h], offs[h]
            b = off // CAP
            for lev in range(LEVELS):
                n, rate = ROWS >> lev, 1 << lev

                @pl.when(level == lev)
                def _():
                    if n > CAP:
                        t = tiles[h * 3 + 1]
                        top, low = t[:CAP], t[CAP:]
                        pick = left_lanes(top.shape)
                        for s in range(2):
                            bins[b + s, 0] = tiles[h * 3 + 2 * s, :CAP, :]
                            bins[b + s, 2] = tiles[h * 3 + 2 * s, CAP:, :]
                        bins[b, 1] = jnp.where(pick, top, roll_half(low))
                        bins[b + 1, 1] = jnp.where(pick, roll_half(top), low)
                    else:
                        row = pl.multiple_of(off % CAP, 8)
                        first = h % rate
                        for j in range(3):
                            src = pl.ds(first, n, stride=rate)
                            bins[b, j, pl.ds(row, n), :] = tiles[h * 3 + j, src, :]

            return carry

        lax.fori_loop(0, HEADS, one, 0)
        out0[...] = bins[:HEADS]

        @pl.when(full[0] > 0)
        def _():
            pltpu.sync_copy(bins.at[pl.ds(HEADS, HEADS)], out1)


def any_spec():
    return pl.BlockSpec(memory_space=pl.ANY)


def smem_spec():
    return pl.BlockSpec(memory_space=pltpu.SMEM)


def vmem_spec():
    return pl.BlockSpec(memory_space=pltpu.VMEM)


BINS = jax.ShapeDtypeStruct((HEADS, 3, CAP, 128), F32)


def pack(levels, counts, x, cot, gain, w_qkv, w_out):
    whole = lambda shape: pl.BlockSpec(shape, lambda g: (0,) * len(shape))
    return pl.pallas_call(
        pack_kernel,
        grid=(3,),
        in_specs=[
            smem_spec(),
            smem_spec(),
            whole((2, ROWS, WIDTH)),
            any_spec(),
            whole((WIDTH,)),
            pl.BlockSpec((WIDTH, WIDTH), lambda g: (0, g)),
            any_spec(),
        ],
        out_specs=[whole(BINS.shape), any_spec(), smem_spec(), smem_spec()],
        out_shape=[
            BINS,
            BINS,
            jax.ShapeDtypeStruct((HEADS,), jnp.int32),
            jax.ShapeDtypeStruct((1,), jnp.int32),
        ],
        scratch_shapes=[
            pltpu.VMEM((HEADS * 3, ROWS, 128), F32),
            pltpu.VMEM((4 * ROWS, WIDTH), BF16),
            pltpu.VMEM((2 * HEADS, 3, CAP, 128), F32),
            pltpu.VMEM((2, ROWS, WIDTH), F32),
            pltpu.VMEM((WIDTH, WIDTH), F32),
            pltpu.SemaphoreType.DMA((2,)),
        ],
        compiler_params=pltpu.CompilerParams(vmem_limit_bytes=60 * MIB),
        cost_estimate=pl.CostEstimate(
            flops=6 * 256 * 768 * 3072, bytes_accessed=14_000_000, transcendentals=0
        ),
        name="project_pack",
    )(levels, counts, x, cot, gain, w_qkv, w_out)


def attend(a, b, block):
    n = a.shape[1]
    q, k = a[:48] * SCALE, a[48:96]
    v = jnp.concatenate([a[96:128], b[:16]], axis=0)
    do = b[16:64]
    qh, ql = split(q)
    kh, kl = split(k)
    vh, vl = split(v)
    dh, dl = split(do)
    pad = jnp.zeros((80, n), F32)
    padh = jnp.zeros((80, n), BF16)
    q3 = jnp.concatenate([qh, qh, ql], axis=0).T
    d3 = jnp.concatenate([dh, dh, dl], axis=0).T
    k3 = jnp.concatenate([kh, kl, kh], axis=0)
    v3 = jnp.concatenate([vh, vl, vh], axis=0)
    v2 = jnp.concatenate([vh, padh, vl, padh], axis=0).T
    k2 = jnp.concatenate([kh, padh, kl, padh], axis=0).T
    do_t = jnp.concatenate([do, pad], axis=0).T
    q2 = jnp.concatenate([qh, ql], axis=0)
    d2 = jnp.concatenate([dh, dl], axis=0)
    outs, dqs = [], []
    dv = jnp.zeros((48, n), F32)
    dk = jnp.zeros((48, n), F32)

    def right(ph, plo, m2):
        both = dot(ph, m2)
        return both[:, :128] + both[:, 128:] + dot(plo, m2[:, :128])

    def left(m2, mh, ph, plo):
        both = dot(m2, ph)
        return both[:48] + both[48:] + dot(mh, plo)

    for i in range(0, n, block):
        r = slice(i, i + block)
        scores = dot(q3[r], k3)
        expo = jnp.exp(scores - jnp.max(scores, axis=-1, keepdims=True))
        prob = expo * (1.0 / jnp.sum(expo, axis=-1, keepdims=True))
        ph, plo = split(prob)
        out = right(ph, plo, v2)
        delta = jnp.sum(out * do_t[r], axis=-1, keepdims=True)
        ds = prob * (dot(d3[r], v3) - delta)
        sh, slo = split(ds)
        outs.append(out)
        dqs.append(right(sh, slo, k2))
        dv = dv + left(d2[:, r], dh[:, r], ph, plo)
        dk = dk + left(q2[:, r], qh[:, r], sh, slo)
    out = jnp.concatenate(outs, axis=0).T[:48]
    dq = jnp.concatenate(dqs, axis=0).T[:48] * SCALE
    return jnp.concatenate([dq, dk, dv[:32]], axis=0), jnp.concatenate([dv[32:], out], axis=0)


def attend_plane(plane, levels, offs, place, buf, out):
    me = place[0] + plane * HEADS

    def one(h, carry):
        level, off = levels[h], offs[h]
        b = off // CAP
        for lev in range(LEVELS):
            n_rows = ROWS >> lev
            wide = n_rows > CAP
            per_slot = max(1, 4 >> lev)
            n_src = 4 << lev if lev < 2 else 16
            n = n_src * n_rows
            half = n // 2
            if wide:
                mine = (b == me) | (b + 1 == me)
            else:
                mine = b == me

            @pl.when((level == lev) & mine)
            def _():
                def unit(u, inner):
                    if wide:
                        src = pl.ds(u * n_src, n_src)
                        a = [buf[src, j].reshape(half, 128) for j in (0, 2)]
                        t = buf[src, 1].reshape(half, 128).T
                        ra, rb = attend(
                            jnp.concatenate(a, axis=0).T,
                            jnp.concatenate([t[:64], t[64:]], axis=1),
                            min(n, BLOCK),
                        )
                        ra = ra.T
                        rb = jnp.concatenate([rb[:, :half], rb[:, half:]], axis=0).T
                        out[src, 0] = ra[:half].reshape(n_src, CAP, 128)
                        out[src, 2] = ra[half:].reshape(n_src, CAP, 128)
                        out[src, 1] = rb.reshape(n_src, CAP, 128)
                    else:
                        row = pl.multiple_of(off % CAP, 8)
                        slot, seg = u // per_slot, u % per_slot
                        src = pl.ds(seg * n_src, n_src)
                        rows = pl.ds(row, n_rows)
                        a = buf[src, 2 * slot, rows, :].reshape(n, 128).T
                        t = buf[src, 1, rows, :].reshape(n, 128).T
                        t = jnp.where(slot == 0, t[:64], t[64:])
                        ra, rb = attend(a, t, min(n, BLOCK))
                        out[src, 2 * slot, rows, :] = ra.T.reshape(n_src, n_rows, 128)
                        rb = jnp.concatenate([rb, rb], axis=0).T.reshape(n_src, n_rows, 128)
                        lane = lax.broadcasted_iota(jnp.int32, rb.shape, 2)
                        keep = (lane >= 64) != (slot == 1)
                        out[src, 1, rows, :] = jnp.where(keep, out[src, 1, rows, :], rb)
                    return inner

                lax.fori_loop(0, per_slot if wide else 2 * per_slot, unit, 0)

        return carry

    lax.fori_loop(0, HEADS, one, 0)


def attend_kernel(levels, offs, full, place, in0, far_in, out0, far_out, in1, out1):
    attend_plane(0, levels, offs, place, in0, out0)

    @pl.when(full[0] > 0)
    def _():
        pltpu.sync_copy(far_in, in1)
        attend_plane(1, levels, offs, place, in1, out1)
        pltpu.sync_copy(out1, far_out)


def attention(levels, offs, full, place, in0, in1):
    return pl.pallas_call(
        attend_kernel,
        in_specs=[smem_spec()] * 4 + [vmem_spec(), any_spec()],
        out_specs=[vmem_spec(), any_spec()],
        out_shape=[BINS, BINS],
        scratch_shapes=[pltpu.VMEM(BINS.shape, F32)] * 2,
        compiler_params=pltpu.CompilerParams(vmem_limit_bytes=14 * MIB),
        cost_estimate=pl.CostEstimate(
            flops=10_000_000_000, bytes_accessed=6_000_000, transcendentals=1_000_000
        ),
        name="attention",
    )(levels, offs, full, place, in0, in1)


def unpack(levels, offs, full, in0, far, in1, tiles):
    @pl.when(full[0] > 0)
    def _():
        pltpu.sync_copy(far, in1)

    tiles[...] = jnp.zeros_like(tiles)

    def one(h, carry):
        level, off = levels[h], offs[h]
        b = off // CAP

        def load(b, *at):
            dev = b % HEADS
            return jnp.where(b < HEADS, in0[(dev, *at)], in1[(dev, *at)])

        for lev in range(LEVELS):
            n, rate = ROWS >> lev, 1 << lev

            @pl.when(level == lev)
            def _():
                if n > CAP:
                    pick = left_lanes((CAP, 128))
                    for s in range(2):
                        tiles[h * 3 + 2 * s, :CAP, :] = load(b + s, 0)
                        tiles[h * 3 + 2 * s, CAP:, :] = load(b + s, 2)
                    b0, b1 = load(b, 1), load(b + 1, 1)
                    tiles[h * 3 + 1, :CAP, :] = jnp.where(pick, b0, roll_half(b1))
                    tiles[h * 3 + 1, CAP:, :] = jnp.where(pick, roll_half(b0), b1)
                else:
                    row = pl.multiple_of(off % CAP, 8)
                    for j in range(3):
                        to = pl.ds(h % rate, n, stride=rate)
                        tiles[h * 3 + j, to, :] = load(b, j, pl.ds(row, n), slice(None))

        return carry

    lax.fori_loop(0, HEADS, one, 0)


def head_piece(tiles, h, s, which):
    if which < 2:
        return tiles[h * 3 + 2 * s][:, HDIM * which : HDIM * (which + 1)]
    tail = tiles[h * 3 + 1][:, 64 * s : 64 * (s + 1)]
    if which == 2:
        return jnp.concatenate([tiles[h * 3 + 2 * s][:, 96:], tail[:, :16]], axis=1)
    return tail[:, 16:]


def columns(tiles, pairs):
    return jnp.concatenate(
        [
            jnp.concatenate([head_piece(tiles, h, s, which) for which, h in pairs], axis=1)
            for s in range(2)
        ],
        axis=0,
    )


def prepare_kernel(counts, place, xa, xb, ca, cb, gain, n2, m2):
    core = place[0] % 2
    live = live_rows(counts)
    for t, (x, cot) in enumerate(((xa, ca), (xb, cb))):
        tok = slice(2 * ROWS * t, 2 * ROWS * (t + 1))
        xhat, _ = normalise(x[...].reshape(2 * ROWS, WIDTH))
        for part, value in enumerate(split(xhat * gain[...][None])):
            n2[part, tok] = value
        masked = cot[...].reshape(2 * ROWS, WIDTH) * live
        for c in range(2):

            @pl.when(core == c)
            def _():
                mine = [masked[:, HDIM * (2 * j + c) : HDIM * (2 * j + c + 1)] for j in range(8)]
                for part, value in enumerate(split(jnp.concatenate(mine, axis=1).T)):
                    m2[part, :, tok] = value


def prepare(counts, place, xa, xb, ca, cb, gain):
    return pl.pallas_call(
        prepare_kernel,
        in_specs=[smem_spec()] * 2 + [vmem_spec()] * 5,
        out_specs=[vmem_spec()] * 2,
        out_shape=[
            jax.ShapeDtypeStruct((2, 4 * ROWS, WIDTH), BF16),
            jax.ShapeDtypeStruct((2, WIDTH // 2, 4 * ROWS), BF16),
        ],
        compiler_params=pltpu.CompilerParams(vmem_limit_bytes=60 * MIB),
        cost_estimate=pl.CostEstimate(
            flops=2_000_000_000, bytes_accessed=6_000_000, transcendentals=0
        ),
        name="prepare",
    )(counts, place, xa, xb, ca, cb, gain)


def grad_kernel(
    levels, offs, full, place, a0, a1, b0, b1, n2, m2,
    z_own, z_up, z_down, z_right, z_left, y_own, y_up, y_down, y_right, y_left,
    far, tiles, left, o2, rows,
):
    core, z_me, y_me = place[0] % 2, place[0] // 4, place[1]
    for t, (in0, in1) in enumerate(((a0, a1), (b0, b1))):
        tok = slice(2 * ROWS * t, 2 * ROWS * (t + 1))
        unpack(levels, offs, full, in0, in1, far, tiles)
        attended = columns(tiles, [(3, h) for h in range(HEADS)])
        for part, value in enumerate(split(attended)):
            o2[part, tok] = value
        for c in range(2):

            @pl.when(core == c)
            def _():
                for j in range(0, 8, 2):
                    at = [3 * (2 * (j + i // 3) + c) + i % 3 for i in range(6)]
                    value = columns(tiles, [(p // HEADS, p % HEADS) for p in at])
                    for part, piece in enumerate(split(value.T)):
                        left[part, 144 * j : 144 * (j + 2), tok] = piece

    for i in range(0, WIDTH, 256):
        cols = slice(i, i + 256)
        nh, nl = n2[0, :, cols], n2[1, :, cols]
        grad = dot(left[0], nh) + dot(left[1], nh) + dot(left[0], nl)
        oh, ol = o2[0, :, cols], o2[1, :, cols]
        out = dot(m2[0], oh) + dot(m2[1], oh) + dot(m2[0], ol)
        for j in range(8):
            rows[j, :144, cols] = grad[144 * j : 144 * (j + 1)]
            rows[j, 144:, cols] = out[HDIM * j : HDIM * (j + 1)]

    def z_part(k, xh):
        return rows[(z_me + k) % 4 * 2 + xh, :96, :]

    for xh in range(2):
        z_own[xh] = z_part(0, xh)
    z_up[0], z_up[1] = z_part(2, 0), z_part(1, 1)
    z_down[0], z_down[1] = z_part(3, 0), z_part(2, 1)
    z_right[...], z_left[...] = z_part(1, 0), z_part(3, 1)

    def y_part(k, z, xh):
        at = pl.multiple_of(96 + 24 * ((y_me + k) % 4), 8)
        return rows[z * 2 + xh, pl.ds(at, 24), :]

    for xh in range(2):
        for z in range(4):
            y_own[z, xh] = y_part(0, z, xh)
        for z in range(2):
            y_up[0, z, xh], y_up[1, z, xh] = y_part(2, z, xh), y_part(1, z + 2, xh)
            y_down[0, z, xh], y_down[1, z, xh] = y_part(3, z, xh), y_part(2, z + 2, xh)
            y_right[z, xh], y_left[z, xh] = y_part(1, z, xh), y_part(3, z + 2, xh)


def grads(levels, offs, full, place, a0, a1, b0, b1, n2, m2):
    zh, yh = (96, WIDTH), (2, 2, 24, WIDTH)
    shapes = [(2, *zh)] * 3 + [zh] * 2 + [(4, *yh[1:])] + [(2, *yh)] * 2 + [yh] * 2
    return pl.pallas_call(
        grad_kernel,
        in_specs=[smem_spec()] * 4 + [vmem_spec(), any_spec()] * 2 + [vmem_spec()] * 2,
        out_specs=[vmem_spec()] * 10,
        out_shape=[jax.ShapeDtypeStruct(shape, F32) for shape in shapes],
        scratch_shapes=[
            pltpu.VMEM(BINS.shape, F32),
            pltpu.VMEM((HEADS * 3, ROWS, 128), F32),
            pltpu.VMEM((2, 8 * 144, 4 * ROWS), BF16),
            pltpu.VMEM((2, 4 * ROWS, WIDTH), BF16),
            pltpu.VMEM((8, 192, WIDTH), F32),
        ],
        compiler_params=pltpu.CompilerParams(vmem_limit_bytes=60 * MIB),
        cost_estimate=pl.CostEstimate(
            flops=6 * 256 * 768 * 3072, bytes_accessed=14_000_000, transcendentals=0
        ),
        name="weight_grads",
    )(levels, offs, full, place, a0, a1, b0, b1, n2, m2)


def outputs_kernel(
    levels, offs, full, counts, in0, in1, x, gain, w_qkv, w_out,
    branch, input_grad, grad_gain, far, tiles,
):
    unpack(levels, offs, full, in0, in1, far, tiles)
    live = live_rows(counts)
    xhat, rstd = normalise(x[...].reshape(2 * ROWS, WIDTH))
    dnormed = jnp.zeros((2 * ROWS, WIDTH), F32)
    for part in range(3):
        value = stack(columns(tiles, [(part, h) for h in range(HEADS)]))
        at = part * WIDTH
        dnormed = dnormed + dot_stack(value, w_qkv[:, at : at + WIDTH], ((1,), (1,)))
    attended2 = stack(columns(tiles, [(3, h) for h in range(HEADS)]))
    branch[...] = (dot_stack(attended2, w_out[...]) * live).reshape(2, ROWS, WIDTH)
    grad_gain[...] = jnp.sum(dnormed * xhat, axis=0)
    dxhat = dnormed * gain[...][None]
    mean_a = jnp.mean(dxhat, axis=-1, keepdims=True)
    mean_b = jnp.mean(dxhat * xhat, axis=-1, keepdims=True)
    input_grad[...] = (rstd * (dxhat - mean_a - xhat * mean_b)).reshape(2, ROWS, WIDTH)


def outputs(levels, offs, full, counts, in0, in1, x, gain, w_qkv, w_out):
    return pl.pallas_call(
        outputs_kernel,
        in_specs=[smem_spec()] * 4 + [vmem_spec(), any_spec()] + [vmem_spec()] * 4,
        out_specs=[vmem_spec()] * 3,
        out_shape=[
            jax.ShapeDtypeStruct((2, ROWS, WIDTH), F32),
            jax.ShapeDtypeStruct((2, ROWS, WIDTH), F32),
            jax.ShapeDtypeStruct((WIDTH,), F32),
        ],
        scratch_shapes=[pltpu.VMEM(BINS.shape, F32), pltpu.VMEM((HEADS * 3, ROWS, 128), F32)],
        compiler_params=pltpu.CompilerParams(vmem_limit_bytes=60 * MIB),
        cost_estimate=pl.CostEstimate(
            flops=6 * 256 * 768 * 3072, bytes_accessed=14_000_000, transcendentals=0
        ),
        name="outputs",
    )(levels, offs, full, counts, in0, in1, x, gain, w_qkv, w_out)


def seq_move(x, step):
    pairs = []
    for i in range(HEADS):
        z, xh, c = step(i // 4, i // 2 % 2, i % 2)
        pairs.append((i, (z % 4) * 4 + xh * 2 + c))
    return lax.ppermute(x, "seq", pairs)


def core_move(x):
    return seq_move(x, lambda z, xh, c: (z, xh, 1 - c))


def z_move(x, k):
    return seq_move(x, lambda z, xh, c: (z + k, xh, c))


def y_move(x, k):
    return lax.ppermute(x, "dp", [(i, (i // 2 + k) % 4 * 2 + i % 2) for i in range(8)])


def x_move(x, step):
    pairs = []
    for d in range(8):
        for s in range(HEADS):
            xh, xl = step(s // 2 % 2, d % 2)
            pairs.append((d * HEADS + s, (d // 2 * 2 + xl) * HEADS + s // 4 * 4 + xh * 2 + s % 2))
    return lax.ppermute(x, ("dp", "seq"), pairs)


def pick(x, index, axis, size=1):
    return lax.dynamic_slice_in_dim(x, index, size, axis)


def ring_send(move, up, down):
    return move(up, 1), move(down, -1)


def ring_sum(move, own, right, left, from_left, from_right):
    right = move(right + from_left[0], 1)
    left = move(left + from_right[1], -1)
    return own[0] + right + from_right[0], own[1] + from_left[1] + left


def reduce_all(parts, finish_outputs):
    place = lax.axis_index("seq")
    z, xh = place // 4, place // 2 % 2
    y = lax.axis_index("dp") // 2
    quarter = 24

    z_own, z_up, z_down, z_right, z_left, y_own, y_up, y_down, y_right, y_left = parts
    sent = ring_send(z_move, z_up, z_down), ring_send(y_move, y_up, y_down)
    done = finish_outputs()
    (z_in, y_in), done = lax.optimization_barrier((sent, done))
    branch, input_grad, gain = done
    zs = jnp.stack(ring_sum(z_move, z_own, z_right, z_left, *z_in))
    y_own = y_own.reshape(2, 2, *y_own.shape[1:])
    ys = jnp.concatenate(ring_sum(y_move, y_own, y_right, y_left, *y_in), axis=0)

    def join(body, extra):
        return jnp.concatenate([body.reshape(-1, WIDTH), extra], axis=0)

    gain = jnp.broadcast_to((gain + core_move(gain))[None], (8, WIDTH))

    zmsg = lambda k: pick(zs, ((y + k) % 4) * quarter, 1, quarter)
    ymsg = lambda k: join(pick(ys, (z + k) % 4, 0), gain)
    z_sum, y_sum = zmsg(0), ymsg(0)
    for k in (1, 2, 3):
        z_sum = z_sum + y_move(zmsg(k), k)
        y_sum = y_sum + z_move(ymsg(k), k)
    y_sum, gain = y_sum[: 2 * quarter], y_sum[2 * quarter :]
    both = jnp.concatenate([z_sum, y_sum.reshape(2, quarter, WIDTH)], axis=1)

    own, other = join(pick(both, xh, 0), gain), join(pick(both, 1 - xh, 0), gain)
    piece = (
        own
        + x_move(own, lambda xh, xl: (xh, 1 - xl))
        + x_move(other, lambda xh, xl: (1 - xh, xl))
        + x_move(other, lambda xh, xl: (1 - xh, 1 - xl))
    )

    pieces = jnp.stack([piece] + [y_move(piece, k) for k in (1, 2, 3)])
    gain = lax.dynamic_slice_in_dim(jnp.sum(pieces[:, 2 * quarter], axis=0), place * HDIM, HDIM)
    order = [pick(pieces, (y - i) % 4, 0)[0] for i in range(4)]
    full = jnp.concatenate(
        [o[:quarter] for o in order] + [o[quarter : 2 * quarter] for o in order], axis=0
    )
    return branch, input_grad, gain, full[: 3 * HDIM].T, full[3 * HDIM :].T


def shards(slides, counts, levels, norm_gain, w_qkv, w_out, cotangent):
    x, cot = slides[0], cotangent[0]
    place = jnp.stack([lax.axis_index("seq"), lax.axis_index("dp") // 2])
    exchange = lambda v: lax.all_to_all(v, "seq", split_axis=0, concat_axis=0, tiled=True)
    x_b, cot_b = core_move(x), core_move(cot)
    sent0, sent1, offs, full = pack(levels, counts, x, cot, norm_gain, w_qkv, w_out)
    more = full[0] > 0
    got0 = exchange(sent0)
    got1 = lax.cond(more, exchange, lambda v: v, sent1)
    n2, m2 = prepare(counts, place, x, x_b, cot, cot_b, norm_gain)
    got0, n2, m2 = lax.optimization_barrier((got0, n2, m2))
    back0, back1 = attention(levels, offs, full, place, got0, got1)
    a0 = exchange(back0)
    b0 = core_move(a0)

    def second(v, unused):
        v = exchange(v)
        return v, core_move(v)

    a1, b1 = lax.cond(more, second, lambda v, unused: (v, unused), back1, got1)
    parts = grads(levels, offs, full, place, a0, a1, b0, b1, n2, m2)
    branch, input_grad, grad_gain, grad_qkv, grad_out = reduce_all(
        parts, lambda: outputs(levels, offs, full, counts, a0, a1, x, norm_gain, w_qkv, w_out)
    )
    return branch[None], input_grad[None], grad_gain, grad_qkv, grad_out


def solution(mesh):
    return jax.shard_map(
        shards,
        mesh=mesh,
        in_specs=(
            P("dp", None, "seq", None),
            P("dp"),
            P(),
            P(),
            P(),
            P(),
            P("dp", None, "seq", None),
        ),
        out_specs=(
            P("dp", None, "seq", None),
            P("dp", None, "seq", None),
            P("seq"),
            P(None, "seq"),
            P(None, "seq"),
        ),
        check_vma=False,
    )
```

```python
from functools import partial

import jax
import jax.numpy as jnp
from jax import lax
from jax.experimental import pallas as pl
from jax.experimental.pallas import tpu as pltpu
from jax.sharding import PartitionSpec as P

HEADS = 16
HDIM = 48
LEVELS = 5
EPS = 1e-05
ROWS = 128
CAP = 64
BLOCK = 512
WIDTH = 768
SCALE = HDIM**-0.5
F32 = jnp.float32
BF16 = jnp.bfloat16
MIB = 1024 * 1024


def split(x):
    hi = x.astype(BF16)
    return hi, (x - hi.astype(F32)).astype(BF16)


def dot(a, b, dims=((1,), (0,))):
    return lax.dot_general(a, b, (dims, ((), ())), preferred_element_type=F32)


def dot_stack(a2, w, dims=((1,), (0,))):
    m = a2.shape[0] // 2
    wh, wl = split(w)
    both = dot(a2, wh, dims)
    return both[:m] + both[m:] + dot(a2[:m], wl, dims)


def stack(x):
    return jnp.concatenate(split(x), axis=0)


def normalise(x):
    mean = jnp.mean(x, axis=-1, keepdims=True)
    centred = x - mean
    rstd = lax.rsqrt(jnp.mean(centred * centred, axis=-1, keepdims=True) + EPS)
    return centred * rstd, rstd


def live_rows(counts):
    rows = lax.broadcasted_iota(jnp.int32, (2 * ROWS, 1), 0)
    return (rows < counts[0] * ROWS).astype(F32)


def roll_half(x):
    return pltpu.roll(x, 64, 1)


def left_lanes(shape):
    return lax.broadcasted_iota(jnp.int32, shape, 1) < 64


def pack_kernel(
    levels, counts, x, far_cot, gain, wqkv, far_wo, out0, out1, offs, full,
    tiles, n2, bins, cot, wo, sems,
):
    g = pl.program_id(0)
    later = [
        pltpu.make_async_copy(far_cot, cot, sems.at[0]),
        pltpu.make_async_copy(far_wo, wo, sems.at[1]),
    ]

    @pl.when(g == 0)
    def _():
        for copy in later:
            copy.start()
        xhat, _ = normalise(x[...].reshape(2 * ROWS, WIDTH))
        n2[...] = stack(xhat * gain[...][None])
        heads = [levels[h] for h in range(HEADS)]
        at, firsts = jnp.int32(0), []
        for lev in range(LEVELS):
            firsts.append(at)
            for level in heads:
                at = at + jnp.where(level == lev, ROWS >> lev, 0)
        full[0] = (at > HEADS * CAP).astype(jnp.int32)
        for h, level in enumerate(heads):
            off = jnp.int32(0)
            for lev in range(LEVELS):
                here = level == lev
                off = jnp.where(here, firsts[lev], off)
                firsts[lev] = firsts[lev] + jnp.where(here, ROWS >> lev, 0)
            offs[h] = off

    for part in range(3):

        @pl.when(g == part)
        def _():
            value = dot_stack(n2[...], wqkv[...])
            for h in range(HEADS):
                for s in range(2):
                    piece = value[ROWS * s : ROWS * (s + 1), HDIM * h : HDIM * (h + 1)]
                    if part < 2:
                        tiles[h * 3 + 2 * s, :, HDIM * part : HDIM * (part + 1)] = piece
                    else:
                        tiles[h * 3 + 2 * s, :, 96:] = piece[:, :32]
                        tiles[h * 3 + 1, :, 64 * s : 64 * s + 16] = piece[:, 32:]

    @pl.when(g == 2)
    def _():
        for copy in later:
            copy.wait()
        c2 = stack(cot[...].reshape(2 * ROWS, WIDTH) * live_rows(counts))
        do = dot_stack(c2, wo[...], ((1,), (1,)))
        for h in range(HEADS):
            for s in range(2):
                piece = do[ROWS * s : ROWS * (s + 1), HDIM * h : HDIM * (h + 1)]
                tiles[h * 3 + 1, :, 64 * s + 16 : 64 * (s + 1)] = piece

        def one(h, carry):
            level, off = levels[h], offs[h]
            b = off // CAP
            for lev in range(LEVELS):
                n, rate = ROWS >> lev, 1 << lev

                @pl.when(level == lev)
                def _():
                    if n > CAP:
                        t = tiles[h * 3 + 1]
                        top, low = t[:CAP], t[CAP:]
                        pick = left_lanes(top.shape)
                        for s in range(2):
                            bins[b + s, 0] = tiles[h * 3 + 2 * s, :CAP, :]
                            bins[b + s, 2] = tiles[h * 3 + 2 * s, CAP:, :]
                        bins[b, 1] = jnp.where(pick, top, roll_half(low))
                        bins[b + 1, 1] = jnp.where(pick, roll_half(top), low)
                    else:
                        row = pl.multiple_of(off % CAP, 8)
                        first = h % rate
                        for j in range(3):
                            src = pl.ds(first, n, stride=rate)
                            bins[b, j, pl.ds(row, n), :] = tiles[h * 3 + j, src, :]

            return carry

        lax.fori_loop(0, HEADS, one, 0)
        out0[...] = bins[:HEADS]

        @pl.when(full[0] > 0)
        def _():
            pltpu.sync_copy(bins.at[pl.ds(HEADS, HEADS)], out1)


def any_spec():
    return pl.BlockSpec(memory_space=pl.ANY)


def smem_spec():
    return pl.BlockSpec(memory_space=pltpu.SMEM)


def vmem_spec():
    return pl.BlockSpec(memory_space=pltpu.VMEM)


BINS = jax.ShapeDtypeStruct((HEADS, 3, CAP, 128), F32)


def pack(levels, counts, x, cot, gain, w_qkv, w_out):
    whole = lambda shape: pl.BlockSpec(shape, lambda g: (0,) * len(shape))
    return pl.pallas_call(
        pack_kernel,
        grid=(3,),
        in_specs=[
            smem_spec(),
            smem_spec(),
            whole((2, ROWS, WIDTH)),
            any_spec(),
            whole((WIDTH,)),
            pl.BlockSpec((WIDTH, WIDTH), lambda g: (0, g)),
            any_spec(),
        ],
        out_specs=[whole(BINS.shape), any_spec(), smem_spec(), smem_spec()],
        out_shape=[
            BINS,
            BINS,
            jax.ShapeDtypeStruct((HEADS,), jnp.int32),
            jax.ShapeDtypeStruct((1,), jnp.int32),
        ],
        scratch_shapes=[
            pltpu.VMEM((HEADS * 3, ROWS, 128), F32),
            pltpu.VMEM((4 * ROWS, WIDTH), BF16),
            pltpu.VMEM((2 * HEADS, 3, CAP, 128), F32),
            pltpu.VMEM((2, ROWS, WIDTH), F32),
            pltpu.VMEM((WIDTH, WIDTH), F32),
            pltpu.SemaphoreType.DMA((2,)),
        ],
        compiler_params=pltpu.CompilerParams(vmem_limit_bytes=60 * MIB),
        cost_estimate=pl.CostEstimate(
            flops=6 * 256 * 768 * 3072, bytes_accessed=14_000_000, transcendentals=0
        ),
        name="project_pack",
    )(levels, counts, x, cot, gain, w_qkv, w_out)


def attend(a, b, block):
    n = a.shape[1]
    q, k = a[:48] * SCALE, a[48:96]
    v = jnp.concatenate([a[96:128], b[:16]], axis=0)
    do = b[16:64]
    qh, ql = split(q)
    kh, kl = split(k)
    vh, vl = split(v)
    dh, dl = split(do)
    pad = jnp.zeros((80, n), F32)
    padh = jnp.zeros((80, n), BF16)
    q3 = jnp.concatenate([qh, qh, ql], axis=0).T
    d3 = jnp.concatenate([dh, dh, dl], axis=0).T
    k3 = jnp.concatenate([kh, kl, kh], axis=0)
    v3 = jnp.concatenate([vh, vl, vh], axis=0)
    v2 = jnp.concatenate([vh, padh, vl, padh], axis=0).T
    k2 = jnp.concatenate([kh, padh, kl, padh], axis=0).T
    do_t = jnp.concatenate([do, pad], axis=0).T
    q2 = jnp.concatenate([qh, ql], axis=0)
    d2 = jnp.concatenate([dh, dl], axis=0)
    outs, dqs = [], []
    dv = jnp.zeros((48, n), F32)
    dk = jnp.zeros((48, n), F32)

    def right(ph, plo, m2):
        both = dot(ph, m2)
        return both[:, :128] + both[:, 128:] + dot(plo, m2[:, :128])

    def left(m2, mh, ph, plo):
        both = dot(m2, ph)
        return both[:48] + both[48:] + dot(mh, plo)

    for i in range(0, n, block):
        r = slice(i, i + block)
        scores = dot(q3[r], k3)
        expo = jnp.exp(scores - jnp.max(scores, axis=-1, keepdims=True))
        prob = expo * (1.0 / jnp.sum(expo, axis=-1, keepdims=True))
        ph, plo = split(prob)
        out = right(ph, plo, v2)
        delta = jnp.sum(out * do_t[r], axis=-1, keepdims=True)
        ds = prob * (dot(d3[r], v3) - delta)
        sh, slo = split(ds)
        outs.append(out)
        dqs.append(right(sh, slo, k2))
        dv = dv + left(d2[:, r], dh[:, r], ph, plo)
        dk = dk + left(q2[:, r], qh[:, r], sh, slo)
    out = jnp.concatenate(outs, axis=0).T[:48]
    dq = jnp.concatenate(dqs, axis=0).T[:48] * SCALE
    return jnp.concatenate([dq, dk, dv[:32]], axis=0), jnp.concatenate([dv[32:], out], axis=0)


def attend_plane(plane, levels, offs, place, buf, out):
    me = place[0] + plane * HEADS

    def one(h, carry):
        level, off = levels[h], offs[h]
        b = off // CAP
        for lev in range(LEVELS):
            n_rows = ROWS >> lev
            wide = n_rows > CAP
            per_slot = max(1, 4 >> lev)
            n_src = 4 << lev if lev < 2 else 16
            n = n_src * n_rows
            half = n // 2
            if wide:
                mine = (b == me) | (b + 1 == me)
            else:
                mine = b == me

            @pl.when((level == lev) & mine)
            def _():
                def unit(u, inner):
                    if wide:
                        src = pl.ds(u * n_src, n_src)
                        a = [buf[src, j].reshape(half, 128) for j in (0, 2)]
                        t = buf[src, 1].reshape(half, 128).T
                        ra, rb = attend(
                            jnp.concatenate(a, axis=0).T,
                            jnp.concatenate([t[:64], t[64:]], axis=1),
                            min(n, BLOCK),
                        )
                        ra = ra.T
                        rb = jnp.concatenate([rb[:, :half], rb[:, half:]], axis=0).T
                        out[src, 0] = ra[:half].reshape(n_src, CAP, 128)
                        out[src, 2] = ra[half:].reshape(n_src, CAP, 128)
                        out[src, 1] = rb.reshape(n_src, CAP, 128)
                    else:
                        row = pl.multiple_of(off % CAP, 8)
                        slot, seg = u // per_slot, u % per_slot
                        src = pl.ds(seg * n_src, n_src)
                        rows = pl.ds(row, n_rows)
                        a = buf[src, 2 * slot, rows, :].reshape(n, 128).T
                        t = buf[src, 1, rows, :].reshape(n, 128).T
                        t = jnp.where(slot == 0, t[:64], t[64:])
                        ra, rb = attend(a, t, min(n, BLOCK))
                        out[src, 2 * slot, rows, :] = ra.T.reshape(n_src, n_rows, 128)
                        rb = jnp.concatenate([rb, rb], axis=0).T.reshape(n_src, n_rows, 128)
                        lane = lax.broadcasted_iota(jnp.int32, rb.shape, 2)
                        keep = (lane >= 64) != (slot == 1)
                        out[src, 1, rows, :] = jnp.where(keep, out[src, 1, rows, :], rb)
                    return inner

                lax.fori_loop(0, per_slot if wide else 2 * per_slot, unit, 0)

        return carry

    lax.fori_loop(0, HEADS, one, 0)


def attend_kernel(levels, offs, full, place, in0, far_in, out0, far_out, in1, out1):
    attend_plane(0, levels, offs, place, in0, out0)

    @pl.when(full[0] > 0)
    def _():
        pltpu.sync_copy(far_in, in1)
        attend_plane(1, levels, offs, place, in1, out1)
        pltpu.sync_copy(out1, far_out)


def attention(levels, offs, full, place, in0, in1):
    return pl.pallas_call(
        attend_kernel,
        in_specs=[smem_spec()] * 4 + [vmem_spec(), any_spec()],
        out_specs=[vmem_spec(), any_spec()],
        out_shape=[BINS, BINS],
        scratch_shapes=[pltpu.VMEM(BINS.shape, F32)] * 2,
        compiler_params=pltpu.CompilerParams(vmem_limit_bytes=14 * MIB),
        cost_estimate=pl.CostEstimate(
            flops=10_000_000_000, bytes_accessed=6_000_000, transcendentals=1_000_000
        ),
        name="attention",
    )(levels, offs, full, place, in0, in1)


def unpack(levels, offs, full, in0, far, in1, tiles):
    @pl.when(full[0] > 0)
    def _():
        pltpu.sync_copy(far, in1)

    tiles[...] = jnp.zeros_like(tiles)

    def one(h, carry):
        level, off = levels[h], offs[h]
        b = off // CAP

        def load(b, *at):
            dev = b % HEADS
            return jnp.where(b < HEADS, in0[(dev, *at)], in1[(dev, *at)])

        for lev in range(LEVELS):
            n, rate = ROWS >> lev, 1 << lev

            @pl.when(level == lev)
            def _():
                if n > CAP:
                    pick = left_lanes((CAP, 128))
                    for s in range(2):
                        tiles[h * 3 + 2 * s, :CAP, :] = load(b + s, 0)
                        tiles[h * 3 + 2 * s, CAP:, :] = load(b + s, 2)
                    b0, b1 = load(b, 1), load(b + 1, 1)
                    tiles[h * 3 + 1, :CAP, :] = jnp.where(pick, b0, roll_half(b1))
                    tiles[h * 3 + 1, CAP:, :] = jnp.where(pick, roll_half(b0), b1)
                else:
                    row = pl.multiple_of(off % CAP, 8)
                    for j in range(3):
                        to = pl.ds(h % rate, n, stride=rate)
                        tiles[h * 3 + j, to, :] = load(b, j, pl.ds(row, n), slice(None))

        return carry

    lax.fori_loop(0, HEADS, one, 0)


def head_piece(tiles, h, s, which):
    if which < 2:
        return tiles[h * 3 + 2 * s][:, HDIM * which : HDIM * (which + 1)]
    tail = tiles[h * 3 + 1][:, 64 * s : 64 * (s + 1)]
    if which == 2:
        return jnp.concatenate([tiles[h * 3 + 2 * s][:, 96:], tail[:, :16]], axis=1)
    return tail[:, 16:]


def columns(tiles, pairs):
    return jnp.concatenate(
        [
            jnp.concatenate([head_piece(tiles, h, s, which) for which, h in pairs], axis=1)
            for s in range(2)
        ],
        axis=0,
    )


def prepare_kernel(counts, place, xa, xb, ca, cb, gain, n2, m2):
    core = place[0] % 2
    live = live_rows(counts)
    for t, (x, cot) in enumerate(((xa, ca), (xb, cb))):
        tok = slice(2 * ROWS * t, 2 * ROWS * (t + 1))
        xhat, _ = normalise(x[...].reshape(2 * ROWS, WIDTH))
        for part, value in enumerate(split(xhat * gain[...][None])):
            n2[part, tok] = value
        masked = cot[...].reshape(2 * ROWS, WIDTH) * live
        for c in range(2):

            @pl.when(core == c)
            def _():
                mine = [masked[:, HDIM * (2 * j + c) : HDIM * (2 * j + c + 1)] for j in range(8)]
                for part, value in enumerate(split(jnp.concatenate(mine, axis=1).T)):
                    m2[part, :, tok] = value


def prepare(counts, place, xa, xb, ca, cb, gain):
    return pl.pallas_call(
        prepare_kernel,
        in_specs=[smem_spec()] * 2 + [vmem_spec()] * 5,
        out_specs=[vmem_spec()] * 2,
        out_shape=[
            jax.ShapeDtypeStruct((2, 4 * ROWS, WIDTH), BF16),
            jax.ShapeDtypeStruct((2, WIDTH // 2, 4 * ROWS), BF16),
        ],
        compiler_params=pltpu.CompilerParams(vmem_limit_bytes=60 * MIB),
        cost_estimate=pl.CostEstimate(
            flops=2_000_000_000, bytes_accessed=6_000_000, transcendentals=0
        ),
        name="prepare",
    )(counts, place, xa, xb, ca, cb, gain)


def grad_kernel(
    levels, offs, full, place, a0, a1, far_b0, b1, far_n2, far_m2,
    z_own, z_up, z_down, z_right, z_left, y_own, y_up, y_down, y_right, y_left,
    far, tiles, left, o2, outs, rows, b0, n2, m2, sems, out_sems,
):
    core, z_me, y_me = place[0] % 2, place[0] // 4, place[1]
    later = [
        pltpu.make_async_copy(far_b0, b0, sems.at[0]),
        pltpu.make_async_copy(far_n2, n2, sems.at[1]),
        pltpu.make_async_copy(far_m2, m2, sems.at[2]),
    ]
    for copy in later:
        copy.start()
    for t, (in0, in1) in enumerate(((a0, a1), (b0, b1))):
        if t == 1:
            later[0].wait()
        tok = slice(2 * ROWS * t, 2 * ROWS * (t + 1))
        unpack(levels, offs, full, in0, in1, far, tiles)
        attended = columns(tiles, [(3, h) for h in range(HEADS)])
        for part, value in enumerate(split(attended)):
            o2[part, tok] = value
        for c in range(2):

            @pl.when(core == c)
            def _():
                for j in range(0, 8, 2):
                    at = [3 * (2 * (j + i // 3) + c) + i % 3 for i in range(6)]
                    value = columns(tiles, [(p // HEADS, p % HEADS) for p in at])
                    for part, piece in enumerate(split(value.T)):
                        left[part, 144 * j : 144 * (j + 2), tok] = piece

    later[1].wait()
    later[2].wait()
    out = dot(m2[0], o2[0]) + dot(m2[1], o2[0]) + dot(m2[0], o2[1])
    outs[...] = out.reshape(8, HDIM, WIDTH)

    sent = []

    def send(source, target):
        copy = pltpu.make_async_copy(source, target, out_sems.at[len(sent)])
        copy.start()
        sent.append(copy)

    z_to = (
        (z_own.at[0], z_own.at[1]),
        (z_right, z_up.at[1]),
        (z_up.at[0], z_down.at[1]),
        (z_down.at[0], z_left),
    )
    for k in range(4):
        z = (z_me + k) % 4
        some = pl.ds(pl.multiple_of(288 * z, 16), 288)
        hi, lo = left[0, some, :], left[1, some, :]
        grad = dot(hi, n2[0]) + dot(lo, n2[0]) + dot(hi, n2[1])
        for xh in range(2):
            rows[2 * k + xh, :144] = grad[144 * xh : 144 * (xh + 1)]
            rows[2 * k + xh, 144:] = outs[z * 2 + xh]
        for xh in range(2):
            send(rows.at[2 * k + xh, pl.ds(0, 96)], z_to[k][xh])
        if k < 2:
            y_to = (y_own.at[k], y_right.at[k], y_up.at[0, k], y_down.at[0, k])
        else:
            y_to = (y_own.at[k], y_up.at[1, k - 2], y_down.at[1, k - 2], y_left.at[k - 2])
        for ky in range(4):
            at = pl.multiple_of(96 + 24 * ((y_me + ky) % 4), 8)
            send(rows.at[pl.ds(2 * k, 2), pl.ds(at, 24)], y_to[ky])
    for copy in sent:
        copy.wait()


def grads(levels, offs, full, place, a0, a1, b0, b1, n2, m2):
    zh, yh = (96, WIDTH), (2, 2, 24, WIDTH)
    shapes = [(2, *zh)] * 3 + [zh] * 2 + [(4, *yh[1:])] + [(2, *yh)] * 2 + [yh] * 2
    return pl.pallas_call(
        grad_kernel,
        in_specs=[smem_spec()] * 4 + [vmem_spec()] + [any_spec()] * 5,
        out_specs=[any_spec()] * 10,
        out_shape=[jax.ShapeDtypeStruct(shape, F32) for shape in shapes],
        scratch_shapes=[
            pltpu.VMEM(BINS.shape, F32),
            pltpu.VMEM((HEADS * 3, ROWS, 128), F32),
            pltpu.VMEM((2, 8 * 144, 4 * ROWS), BF16),
            pltpu.VMEM((2, 4 * ROWS, WIDTH), BF16),
            pltpu.VMEM((8, HDIM, WIDTH), F32),
            pltpu.VMEM((8, 192, WIDTH), F32),
            pltpu.VMEM(BINS.shape, F32),
            pltpu.VMEM((2, 4 * ROWS, WIDTH), BF16),
            pltpu.VMEM((2, WIDTH // 2, 4 * ROWS), BF16),
            pltpu.SemaphoreType.DMA((3,)),
            pltpu.SemaphoreType.DMA((24,)),
        ],
        compiler_params=pltpu.CompilerParams(vmem_limit_bytes=60 * MIB),
        cost_estimate=pl.CostEstimate(
            flops=6 * 256 * 768 * 3072, bytes_accessed=14_000_000, transcendentals=0
        ),
        name="weight_grads",
    )(levels, offs, full, place, a0, a1, b0, b1, n2, m2)


def outputs_kernel(
    levels, offs, full, counts, in0, in1, x, gain, w_qkv, w_out,
    branch, input_grad, grad_gain, far, tiles,
):
    unpack(levels, offs, full, in0, in1, far, tiles)
    live = live_rows(counts)
    xhat, rstd = normalise(x[...].reshape(2 * ROWS, WIDTH))
    dnormed = jnp.zeros((2 * ROWS, WIDTH), F32)
    for part in range(3):
        value = stack(columns(tiles, [(part, h) for h in range(HEADS)]))
        at = part * WIDTH
        dnormed = dnormed + dot_stack(value, w_qkv[:, at : at + WIDTH], ((1,), (1,)))
    attended2 = stack(columns(tiles, [(3, h) for h in range(HEADS)]))
    branch[...] = (dot_stack(attended2, w_out[...]) * live).reshape(2, ROWS, WIDTH)
    grad_gain[...] = jnp.sum(dnormed * xhat, axis=0)
    dxhat = dnormed * gain[...][None]
    mean_a = jnp.mean(dxhat, axis=-1, keepdims=True)
    mean_b = jnp.mean(dxhat * xhat, axis=-1, keepdims=True)
    input_grad[...] = (rstd * (dxhat - mean_a - xhat * mean_b)).reshape(2, ROWS, WIDTH)


def outputs(levels, offs, full, counts, in0, in1, x, gain, w_qkv, w_out):
    return pl.pallas_call(
        outputs_kernel,
        in_specs=[smem_spec()] * 4 + [vmem_spec(), any_spec()] + [vmem_spec()] * 4,
        out_specs=[vmem_spec()] * 3,
        out_shape=[
            jax.ShapeDtypeStruct((2, ROWS, WIDTH), F32),
            jax.ShapeDtypeStruct((2, ROWS, WIDTH), F32),
            jax.ShapeDtypeStruct((WIDTH,), F32),
        ],
        scratch_shapes=[pltpu.VMEM(BINS.shape, F32), pltpu.VMEM((HEADS * 3, ROWS, 128), F32)],
        compiler_params=pltpu.CompilerParams(vmem_limit_bytes=60 * MIB),
        cost_estimate=pl.CostEstimate(
            flops=6 * 256 * 768 * 3072, bytes_accessed=14_000_000, transcendentals=0
        ),
        name="outputs",
    )(levels, offs, full, counts, in0, in1, x, gain, w_qkv, w_out)


def seq_move(x, step):
    pairs = []
    for i in range(HEADS):
        z, xh, c = step(i // 4, i // 2 % 2, i % 2)
        pairs.append((i, (z % 4) * 4 + xh * 2 + c))
    return lax.ppermute(x, "seq", pairs)


def core_move(x):
    return seq_move(x, lambda z, xh, c: (z, xh, 1 - c))


def z_move(x, k):
    return seq_move(x, lambda z, xh, c: (z + k, xh, c))


def y_move(x, k):
    return lax.ppermute(x, "dp", [(i, (i // 2 + k) % 4 * 2 + i % 2) for i in range(8)])


def x_move(x, step):
    pairs = []
    for d in range(8):
        for s in range(HEADS):
            xh, xl = step(s // 2 % 2, d % 2)
            pairs.append((d * HEADS + s, (d // 2 * 2 + xl) * HEADS + s // 4 * 4 + xh * 2 + s % 2))
    return lax.ppermute(x, ("dp", "seq"), pairs)


def pick(x, index, axis, size=1):
    return lax.dynamic_slice_in_dim(x, index, size, axis)


def ring_send(move, up, down):
    return move(up, 1), move(down, -1)


def ring_sum(move, own, right, left, from_left, from_right):
    right = move(right + from_left[0], 1)
    left = move(left + from_right[1], -1)
    return own[0] + right + from_right[0], own[1] + from_left[1] + left


def reduce_all(parts, finish_outputs):
    place = lax.axis_index("seq")
    xh = place // 2 % 2
    y = lax.axis_index("dp") // 2
    quarter = 24

    z_own, z_up, z_down, z_right, z_left, y_own, y_up, y_down, y_right, y_left = parts
    sent = ring_send(z_move, z_up, z_down), ring_send(y_move, y_up, y_down)
    done = finish_outputs()
    (z_in, y_in), done = lax.optimization_barrier((sent, done))
    branch, input_grad, gain = done
    zs = jnp.stack(ring_sum(z_move, z_own, z_right, z_left, *z_in))
    y_own = y_own.reshape(2, 2, *y_own.shape[1:])
    ys = jnp.concatenate(ring_sum(y_move, y_own, y_right, y_left, *y_in), axis=0)

    def join(body, extra):
        return jnp.concatenate([body.reshape(-1, WIDTH), extra], axis=0)

    gain = jnp.broadcast_to((gain + core_move(gain))[None], (8, WIDTH))

    zmsg = lambda k: pick(zs, ((y + k) % 4) * quarter, 1, quarter)
    ymsg = lambda k: join(ys[k], gain)
    z_sum, y_sum = zmsg(0), ymsg(0)
    for k in (1, 2, 3):
        z_sum = z_sum + y_move(zmsg(k), k)
        y_sum = y_sum + z_move(ymsg(k), k)
    y_sum, gain = y_sum[: 2 * quarter], y_sum[2 * quarter :]
    both = jnp.concatenate([z_sum, y_sum.reshape(2, quarter, WIDTH)], axis=1)

    own, other = join(pick(both, xh, 0), gain), join(pick(both, 1 - xh, 0), gain)
    piece = (
        own
        + x_move(own, lambda xh, xl: (xh, 1 - xl))
        + x_move(other, lambda xh, xl: (1 - xh, xl))
        + x_move(other, lambda xh, xl: (1 - xh, 1 - xl))
    )

    pieces = jnp.stack([piece] + [y_move(piece, k) for k in (1, 2, 3)])
    gain = lax.dynamic_slice_in_dim(jnp.sum(pieces[:, 2 * quarter], axis=0), place * HDIM, HDIM)
    order = [pick(pieces, (y - i) % 4, 0)[0] for i in range(4)]
    full = jnp.concatenate(
        [o[:quarter] for o in order] + [o[quarter : 2 * quarter] for o in order], axis=0
    )
    return branch, input_grad, gain, full[: 3 * HDIM].T, full[3 * HDIM :].T


def shards(slides, counts, levels, norm_gain, w_qkv, w_out, cotangent):
    x, cot = slides[0], cotangent[0]
    place = jnp.stack([lax.axis_index("seq"), lax.axis_index("dp") // 2])
    exchange = lambda v: lax.all_to_all(v, "seq", split_axis=0, concat_axis=0, tiled=True)
    x_b, cot_b = core_move(x), core_move(cot)
    sent0, sent1, offs, full = pack(levels, counts, x, cot, norm_gain, w_qkv, w_out)
    more = full[0] > 0
    got0 = exchange(sent0)
    got1 = lax.cond(more, exchange, lambda v: v, sent1)
    n2, m2 = prepare(counts, place, x, x_b, cot, cot_b, norm_gain)
    got0, n2, m2 = lax.optimization_barrier((got0, n2, m2))
    back0, back1 = attention(levels, offs, full, place, got0, got1)
    a0 = exchange(back0)
    b0 = core_move(a0)

    def second(v, unused):
        v = exchange(v)
        return v, core_move(v)

    a1, b1 = lax.cond(more, second, lambda v, unused: (v, unused), back1, got1)
    parts = grads(levels, offs, full, place, a0, a1, b0, b1, n2, m2)
    branch, input_grad, grad_gain, grad_qkv, grad_out = reduce_all(
        parts, lambda: outputs(levels, offs, full, counts, a0, a1, x, norm_gain, w_qkv, w_out)
    )
    return branch[None], input_grad[None], grad_gain, grad_qkv, grad_out


def solution(mesh):
    return jax.shard_map(
        shards,
        mesh=mesh,
        in_specs=(
            P("dp", None, "seq", None),
            P("dp"),
            P(),
            P(),
            P(),
            P(),
            P("dp", None, "seq", None),
        ),
        out_specs=(
            P("dp", None, "seq", None),
            P("dp", None, "seq", None),
            P("seq"),
            P(None, "seq"),
            P(None, "seq"),
        ),
        check_vma=False,
    )
```
